32 devices in a mesh: grp: 4 (over z), narrow: 8 (over y, x, core).
Axes of the slice: x: 2, y: 2, z: 4, core: 2. Of those that a mesh axis runs over, the one named last changes fastest.
Arguments:
- panel: bfloat16 [64, 57344], P(None, ('grp', 'narrow')), may hold values from -6 to 6
- tiles: bfloat16 [16384, 128, 128], P(('grp', 'narrow')), may hold values from -0.125 to 0.125
- tile_row: int32 [16384], P(('grp', 'narrow')), may hold values from 0 to 447, as said below
- tile_col: int32 [16384], P(('grp', 'narrow')), may hold values from 0 to 447, as said below
- tile_count: int32 [32], P(('grp', 'narrow')), may hold values from 128 to 512, as said below
Outputs:
- filtered: bfloat16 [64, 57344], P(None, ('grp', 'narrow'))
- normal_image: float32 [64, 57344], P(None, ('grp', 'narrow'))
The draws below stay inside these ranges and needn't reach their ends.
Inputs may be any that keep to these rules, and one draw needn't show every extreme that they name: tile_row of a slot on a device of grp index g lies in g * 112 .. (g + 1) * 112 - 1. tile_col of a slot on a device of grp index g lies in (g - 1) * 112 .. (g + 1) * 112 - 1, and in g * 112 .. for g = 0. `tile_count`: some device holds 512 live slots.
All inputs are finite; a program needn't handle non-finite values.
Results may differ from the reference program's by a relative error of at most 0.009.
Values may be sent and summed in bfloat16 or wider, within the bound.
A program may use at most 128 MiB of HBM per device.

```python
import jax
import jax.numpy as jnp
from jax import lax

COLS = 64
TILE = 128
NBD = 14
TILE_DEV = 512
NBG = 112
NPIX = 57344
SLOTS = 16384
N_NARROW = 8
DEVICES = 32


def slot_group(count):
    return jnp.arange(count) // TILE_DEV // N_NARROW


def draw_tile_row(key, part):
    group = slot_group(SLOTS)
    offset = jax.random.randint(jax.random.fold_in(key, 11), (SLOTS,), 0, NBG)
    return (group * NBG + offset).astype(jnp.int32)


def draw_tile_col(key, part):
    group = slot_group(SLOTS)
    offset = jax.random.randint(jax.random.fold_in(key, 23), (SLOTS,), 0, NBG)
    before = jax.random.randint(jax.random.fold_in(key, 37), (SLOTS,), 0, 2)
    before = jnp.where(group > 0, before, 0)
    return (group * NBG + offset - before * NBG).astype(jnp.int32)


def draw_tile_count(key, part):
    divisor = jax.random.randint(jax.random.fold_in(key, 41), (DEVICES,), 1, 5)
    counts = TILE_DEV // divisor
    fullest = jax.random.randint(jax.random.fold_in(key, 53), (), 0, DEVICES)
    counts = jnp.where(jnp.arange(DEVICES) == fullest, TILE_DEV, counts)
    return counts.astype(jnp.int32)


def level_of(key, dims, shards, least, top_value):
    factor_of, own = 1.0, jax.random.fold_in(key, 6)
    for position, parts in shards:
        steps = jnp.exp(jax.random.uniform(jax.random.fold_in(own, position), (parts,), jnp.float32, least / len(shards), top_value / len(shards)))
        factor_of = factor_of * jnp.repeat(steps, dims[position] // parts).reshape([-1 if axis == position else 1 for axis in range(len(dims))])
    return factor_of


def centred(stream_key, extent, spread, bound, shards=(), held_as=jnp.bfloat16):
    values = spread * jax.random.normal(stream_key, extent, jnp.float32)
    if shards:
        values = values * level_of(stream_key, extent, shards, -0.22, 0.18)
    return jnp.clip(values, -bound, bound).astype(held_as)


def setup_inputs(seed: int = 0) -> dict:
    arg_keys = jax.random.split(jax.random.key(seed), 6)
    panel = centred(arg_keys[0], (COLS, NPIX), 1.0, 6.0, ((1, 32),))
    tiles = centred(arg_keys[1], (SLOTS, TILE, TILE), (TILE * TILE_DEV // (2 * NBD)) ** -0.5, 0.125, ((0, 32),))
    tile_row = draw_tile_row(jax.random.fold_in(arg_keys[5], 71), 0)
    tile_col = draw_tile_col(jax.random.fold_in(arg_keys[5], 71), 0)
    tile_count = draw_tile_count(jax.random.fold_in(arg_keys[5], 71), 0)
    return dict(panel=panel, tiles=tiles, tile_row=tile_row, tile_col=tile_col, tile_count=tile_count)


def reference(panel, tiles, tile_row, tile_col, tile_count):
    cols = panel.shape[0]
    npix = panel.shape[1]
    nblk = npix // TILE
    slots = tiles.shape[0]
    owner = jnp.arange(slots) // TILE_DEV
    live = ((jnp.arange(slots) % TILE_DEV) < tile_count[owner]).astype(jnp.float32)
    groups = slots // TILE_DEV
    part_tiles = tiles.reshape(groups, TILE_DEV, TILE, TILE)
    rows = tile_row.reshape(groups, TILE_DEV)
    columns = tile_col.reshape(groups, TILE_DEV)
    masks = live.reshape(groups, TILE_DEV)
    blocked = panel.reshape(cols, nblk, TILE)

    def forward(acc, item):
        part, rowidx, colidx, mask = item
        pieces = blocked[:, colidx, :].astype(jnp.float32)
        prod = jnp.einsum('kti,tji->ktj', pieces, part.astype(jnp.float32)) * mask[None, :, None]
        return acc.at[:, rowidx, :].add(prod), None

    start = jnp.zeros((cols, nblk, TILE), jnp.float32)
    ysum, _ = lax.scan(forward, start, (part_tiles, rows, columns, masks))
    filtered = ysum.astype(jnp.bfloat16)

    def backward(acc, item):
        part, rowidx, colidx, mask = item
        pieces = filtered[:, rowidx, :].astype(jnp.float32)
        prod = jnp.einsum('ktj,tji->kti', pieces, part.astype(jnp.float32)) * mask[None, :, None]
        return acc.at[:, colidx, :].add(prod), None

    zsum, _ = lax.scan(backward, start, (part_tiles, rows, columns, masks))
    return filtered.reshape(cols, npix), zsum.reshape(cols, npix)
```

```python
import functools

import jax
import jax.numpy as jnp
from jax import lax
from jax.experimental import pallas as pl
from jax.experimental.pallas import tpu as pltpu
from jax.sharding import PartitionSpec as P

MESH = pl.DeviceIdType.MESH
VMEM_LIMIT = 56 * 1024 * 1024
BATCH = 8
ANY = pl.BlockSpec(memory_space=pl.ANY)
VMEM = pl.BlockSpec(memory_space=pltpu.VMEM)


def flip(index, mask):
    bit = 1
    while bit <= mask:
        if mask & bit:
            index = index + bit - 2 * bit * ((index // bit) % 2)
        bit *= 2
    return index


def bits_of(n):
    bits = []
    while 2 ** len(bits) < n:
        bits.append(2 ** len(bits))
    return bits


def spread_orders(n):
    bits = bits_of(n)
    return [bits[1:] + bits[:1], bits[:0:-1] + bits[:1]]


def sum_orders(n):
    bits = bits_of(n)
    return [bits[:1] + bits[1:], bits[:1] + bits[:0:-1]]


def halves_of(nbd):
    return [(0, nbd // 2), (nbd // 2, nbd - nbd // 2)]


def greet(n, group, groups, me, along_grp):
    barrier = pltpu.get_barrier_semaphore()
    bits = bits_of(n)
    for bit in bits:
        pl.semaphore_signal(barrier, inc=1, device_id=(group, flip(me, bit)), device_id_type=MESH)
    if along_grp:
        @pl.when(group > 0)
        def _():
            pl.semaphore_signal(barrier, inc=1, device_id=(group - 1, me), device_id_type=MESH)

        @pl.when(group < groups - 1)
        def _():
            pl.semaphore_signal(barrier, inc=1, device_id=(group + 1, me), device_id_type=MESH)

        ends = jnp.minimum(group, 1) + jnp.minimum(groups - 1 - group, 1)
        pl.semaphore_wait(barrier, len(bits) + ends)
    else:
        pl.semaphore_wait(barrier, len(bits))


def spread_steps(n):
    steps = []
    for half, order in enumerate(spread_orders(n)):
        place = {bit: k for k, bit in enumerate(order)}
        for r in range(n):
            held = [place[bit] for bit in order if r & bit]
            last = max(held) if held else -1
            steps.append((len(held), half, r, order[last + 1:]))
    return [step[1:] for step in sorted(steps, key=lambda s: (s[0], s[2], s[1]))]


def spread_copy(n, nbd, group, me, own, out, base, send, recv, half, r, bit):
    start, size = halves_of(nbd)[half]
    at = pl.ds(base + flip(me, r) * nbd + start, size)
    source = own.at[pl.ds(start, size)] if r == 0 else out.at[at]
    return pltpu.make_async_remote_copy(
        src_ref=source, dst_ref=out.at[at],
        send_sem=send.at[half, r | bit], recv_sem=recv.at[half, r | bit],
        device_id=(group, flip(me, bit)), device_id_type=MESH)


def spread_run(n, nbd, group, me, own, out, base, send, recv, steps, begin):
    copy = functools.partial(spread_copy, n, nbd, group, me, own, out, base, send, recv)
    for half, r, sends in steps:
        if r:
            low = spread_orders(n)[half]
            last = [bit for bit in low if r & bit][-1]
            copy(half, r - last, last).wait_recv()
        for bit in sends:
            copy(half, r, bit).start()


def spread_finish(n, nbd, group, me, own, out, base, send, recv):
    copy = functools.partial(spread_copy, n, nbd, group, me, own, out, base, send, recv)
    for half, r, sends in spread_steps(n):
        for bit in sends:
            copy(half, r, bit).wait_send()


def gather_kernel(n, groups, panel, out, mine, zrecv, send, recv, psend, precv, zsem, lsem):
    group, me = lax.axis_index("grp"), lax.axis_index("narrow")
    nbd = mine.shape[0]
    nbg = n * nbd
    for j in range(nbd):
        mine[j] = panel[:, j * 128:(j + 1) * 128]
    greet(n, group, groups, me, True)

    def zcopy():
        return pltpu.make_async_remote_copy(
            src_ref=mine, dst_ref=zrecv, send_sem=zsem.at[0], recv_sem=zsem.at[1],
            device_id=(group + 1, me), device_id_type=MESH)

    @pl.when(group < groups - 1)
    def _():
        zcopy().start()

    steps = spread_steps(n)
    keep = pltpu.make_async_copy(mine, out.at[pl.ds(nbg + me * nbd, nbd)], lsem.at[0])
    keep.start()
    own_args = (n, nbd, group, me, mine, out, nbg, send, recv)
    prior_args = (n, nbd, group, me, zrecv, out, 0, psend, precv)
    spread_run(*own_args, steps, 0)

    @pl.when(group > 0)
    def _():
        pltpu.make_async_remote_copy(
            src_ref=mine, dst_ref=zrecv, send_sem=zsem.at[0], recv_sem=zsem.at[1],
            device_id=(group - 1, me), device_id_type=MESH).wait_recv()
        kept = pltpu.make_async_copy(zrecv, out.at[pl.ds(me * nbd, nbd)], lsem.at[1])
        kept.start()
        spread_run(*prior_args, steps, 0)
        spread_finish(*prior_args)
        kept.wait()

    spread_finish(*own_args)
    keep.wait()

    @pl.when(group < groups - 1)
    def _():
        zcopy().wait_send()


def gather(n, groups, nbd, panel):
    cols = panel.shape[0]
    nbg = n * nbd
    return pl.pallas_call(
        functools.partial(gather_kernel, n, groups),
        out_shape=jax.ShapeDtypeStruct((2 * nbg, cols, 128), jnp.bfloat16),
        in_specs=[VMEM],
        out_specs=ANY,
        scratch_shapes=[
            pltpu.VMEM((nbd, cols, 128), jnp.bfloat16),
            pltpu.VMEM((nbd, cols, 128), jnp.bfloat16),
            pltpu.SemaphoreType.DMA((2, n)),
            pltpu.SemaphoreType.DMA((2, n)),
            pltpu.SemaphoreType.DMA((2, n)),
            pltpu.SemaphoreType.DMA((2, n)),
            pltpu.SemaphoreType.DMA((2,)),
            pltpu.SemaphoreType.DMA((2,)),
        ],
        compiler_params=pltpu.CompilerParams(
            collective_id=1, has_side_effects=True, vmem_limit_bytes=VMEM_LIMIT),
        name="gather_panel",
    )(panel)


def apply_kernel(block, nin, nout, in_of, out_of, contract, rows, cols, count, src, tiles, out, acc):
    step = pl.program_id(0)
    live = count[0]

    @pl.when(step == 0)
    def _():
        acc[...] = jnp.zeros_like(acc)

    first = step * block
    here = jnp.clip(live - first, 0, block)

    def batch(b, carry):
        prods, places = [], []
        for u in range(BATCH):
            at = b * BATCH + u
            slot = first + at
            prods.append(lax.dot_general(
                src[in_of(rows, cols, slot)], tiles[at], (((1,), (contract,)), ((), ())),
                preferred_element_type=jnp.float32))
            places.append(jnp.where(slot < live, out_of(rows, cols, slot), nout))
        for place, prod in zip(places, prods):
            acc[place] += prod
        return carry

    lax.fori_loop(0, (here + BATCH - 1) // BATCH, batch, 0)

    @pl.when(step == pl.num_programs(0) - 1)
    def _():
        def put(j, carry):
            out[j] = acc[j].astype(out.dtype)
            return carry
        lax.fori_loop(0, nout, put, 0)


def apply_tiles(forward, nbg, src, tiles, tile_row, tile_col, tile_count):
    slots, tile = tiles.shape[:2]
    kcols = src.shape[1]
    block = min(64, slots)
    group = lax.axis_index("grp")
    local_row = tile_row - group * nbg
    local_col = tile_col - (group - 1) * nbg
    by_row = lambda rows, cols, slot: rows[slot]
    by_col = lambda rows, cols, slot: cols[slot]
    nin, nout = (2 * nbg, nbg) if forward else (nbg, 2 * nbg)
    in_of, out_of = (by_col, by_row) if forward else (by_row, by_col)
    return pl.pallas_call(
        functools.partial(apply_kernel, block, nin, nout, in_of, out_of, 1 if forward else 0),
        out_shape=jax.ShapeDtypeStruct((nout, kcols, tile), jnp.bfloat16),
        grid_spec=pltpu.PrefetchScalarGridSpec(
            num_scalar_prefetch=3,
            grid=(slots // block,),
            in_specs=[
                pl.BlockSpec((nin, kcols, tile), lambda i, r, c, n: (0, 0, 0)),
                pl.BlockSpec(
                    (block, tile, tile),
                    lambda i, r, c, n: (jnp.minimum(i, jnp.maximum(n[0] - 1, 0) // block), 0, 0)),
            ],
            out_specs=pl.BlockSpec((nout, kcols, tile), lambda i, r, c, n: (0, 0, 0)),
            scratch_shapes=[pltpu.VMEM((nout + 1, kcols, tile), jnp.float32)],
        ),
        compiler_params=pltpu.CompilerParams(
            dimension_semantics=("arbitrary",), vmem_limit_bytes=VMEM_LIMIT),
        name="apply_forward" if forward else "apply_transposed",
    )(local_row, local_col, tile_count, src, tiles)


class Summed:
    def __init__(self, n, nbd, group, me, part, base, staged, landed, send, recv):
        self.n, self.nbd, self.group, self.me = n, nbd, group, me
        self.part, self.base = part, base
        self.staged, self.landed, self.send, self.recv = staged, landed, send, recv
        self.orders = sum_orders(n)

    def copy(self, half, r):
        order = self.orders[half]
        bit = [b for b in order if r & b][0]
        start, size = halves_of(self.nbd)[half]
        if bit == order[0]:
            source = self.part.at[pl.ds(self.base + flip(self.me, r) * self.nbd + start, size)]
        else:
            source = self.staged.at[r, pl.ds(start, size)]
        return pltpu.make_async_remote_copy(
            src_ref=source, dst_ref=self.landed.at[r, pl.ds(start, size)],
            send_sem=self.send.at[half, r], recv_sem=self.recv.at[half, r],
            device_id=(self.group, flip(self.me, bit)), device_id_type=MESH)

    def sent_at(self, half, stage):
        order = self.orders[half]
        done = sum(order[:stage])
        rest = [r for r in range(self.n) if r & order[stage] and not r & done]

        def needed(r):
            later = [k for k, b in enumerate(order) if r & b and k > stage]
            return later[0] if later else len(order)

        return sorted(rest, key=needed)

    def value(self, half, r, stage, put):
        order = self.orders[half]
        start, size = halves_of(self.nbd)[half]
        for bit in order[:stage]:
            self.copy(half, r | bit).wait_recv()
        first = self.base + flip(self.me, r) * self.nbd
        for j in range(start, start + size):
            total = self.part[first + j].astype(jnp.float32)
            for bit in order[:stage]:
                total = total + self.landed[r | bit, j].astype(jnp.float32)
            put(j, total)

    def stage(self, stage):
        for half in range(2):
            for r in self.sent_at(half, stage):
                if stage:
                    def put(j, total, r=r):
                        self.staged[r, j] = total.astype(jnp.bfloat16)
                    self.value(half, r, stage, put)
                self.copy(half, r).start()

    def finish(self, put):
        for half in range(2):
            self.value(half, 0, len(self.orders[half]), put)

    def drain(self):
        for half in range(2):
            for r in range(1, self.n):
                self.copy(half, r).wait_send()


def reduce_kernel(n, groups, part, filtered, out, mine, staged, landed, send, recv, gsend, grecv, lsem):
    group, me = lax.axis_index("grp"), lax.axis_index("narrow")
    nbd = mine.shape[0]
    greet(n, group, groups, me, False)
    summed = Summed(n, nbd, group, me, part, 0, staged, landed, send, recv)
    for stage in range(len(bits_of(n))):
        summed.stage(stage)

    def put(j, total):
        rounded = total.astype(jnp.bfloat16)
        mine[j] = rounded
        filtered[:, j * 128:(j + 1) * 128] = rounded

    summed.finish(put)
    keep = pltpu.make_async_copy(mine, out.at[pl.ds(me * nbd, nbd)], lsem.at[0])
    keep.start()
    args = (n, nbd, group, me, mine, out, 0, gsend, grecv)
    spread_run(*args, spread_steps(n), 0)
    summed.drain()
    spread_finish(*args)
    keep.wait()


def reduce_rows(n, groups, nbd, part):
    nbg, cols = part.shape[:2]
    return pl.pallas_call(
        functools.partial(reduce_kernel, n, groups),
        out_shape=(
            jax.ShapeDtypeStruct((cols, nbd * 128), jnp.bfloat16),
            jax.ShapeDtypeStruct((nbg, cols, 128), jnp.bfloat16),
        ),
        in_specs=[VMEM],
        out_specs=(VMEM, ANY),
        scratch_shapes=[
            pltpu.VMEM((nbd, cols, 128), jnp.bfloat16),
            pltpu.VMEM((n, nbd, cols, 128), jnp.bfloat16),
            pltpu.VMEM((n, nbd, cols, 128), jnp.bfloat16),
            pltpu.SemaphoreType.DMA((2, n)),
            pltpu.SemaphoreType.DMA((2, n)),
            pltpu.SemaphoreType.DMA((2, n)),
            pltpu.SemaphoreType.DMA((2, n)),
            pltpu.SemaphoreType.DMA((1,)),
        ],
        compiler_params=pltpu.CompilerParams(
            collective_id=2, has_side_effects=True, vmem_limit_bytes=VMEM_LIMIT),
        name="reduce_rows",
    )(part)


def image_kernel(n, groups, part, out, mine, zrecv, pstaged, planded, ostaged, olanded,
                 psend, precv, osend, orecv, zsem):
    group, me = lax.axis_index("grp"), lax.axis_index("narrow")
    nbd = mine.shape[0]
    greet(n, group, groups, me, True)
    prior = Summed(n, nbd, group, me, part, 0, pstaged, planded, psend, precv)
    own = Summed(n, nbd, group, me, part, n * nbd, ostaged, olanded, osend, orecv)

    def zcopy(target):
        return pltpu.make_async_remote_copy(
            src_ref=mine, dst_ref=zrecv, send_sem=zsem.at[0], recv_sem=zsem.at[1],
            device_id=(target, me), device_id_type=MESH)

    for stage in range(len(bits_of(n))):
        @pl.when(group > 0)
        def _():
            prior.stage(stage)
        own.stage(stage)

    @pl.when(group > 0)
    def _():
        def put(j, total):
            mine[j] = total.astype(jnp.bfloat16)
        prior.finish(put)
        zcopy(group - 1).start()

    def put_own(j, total):
        out[:, j * 128:(j + 1) * 128] = total

    own.finish(put_own)

    @pl.when(group < groups - 1)
    def _():
        zcopy(group + 1).wait_recv()
        for j in range(nbd):
            at = slice(j * 128, (j + 1) * 128)
            out[:, at] = out[:, at] + zrecv[j].astype(jnp.float32)

    own.drain()

    @pl.when(group > 0)
    def _():
        prior.drain()
        zcopy(group - 1).wait_send()


def image(n, groups, nbd, part):
    cols = part.shape[1]
    held = pltpu.VMEM((n, nbd, cols, 128), jnp.bfloat16)
    sems = pltpu.SemaphoreType.DMA((2, n))
    piece = pltpu.VMEM((nbd, cols, 128), jnp.bfloat16)
    return pl.pallas_call(
        functools.partial(image_kernel, n, groups),
        out_shape=jax.ShapeDtypeStruct((cols, nbd * 128), jnp.float32),
        in_specs=[VMEM],
        out_specs=VMEM,
        scratch_shapes=[piece, piece, held, held, held, held, sems, sems, sems, sems,
                        pltpu.SemaphoreType.DMA((2,))],
        compiler_params=pltpu.CompilerParams(
            collective_id=3, has_side_effects=True, vmem_limit_bytes=VMEM_LIMIT),
        name="image_sums",
    )(part)


def body(panel, tiles, tile_row, tile_col, tile_count):
    tile = tiles.shape[1]
    nbd = panel.shape[1] // tile
    n, groups = lax.axis_size("narrow"), lax.axis_size("grp")
    nbg = nbd * n
    both = gather(n, groups, nbd, panel)
    part = apply_tiles(True, nbg, both, tiles, tile_row, tile_col, tile_count)
    filtered, rows = reduce_rows(n, groups, nbd, part)
    sums = apply_tiles(False, nbg, rows, tiles, tile_row, tile_col, tile_count)
    return filtered, image(n, groups, nbd, sums)


def solution(mesh):
    spread = P(("grp", "narrow"))
    columns = P(None, ("grp", "narrow"))
    return jax.shard_map(
        body,
        mesh=mesh,
        in_specs=(columns, P(("grp", "narrow"), None, None), spread, spread, spread),
        out_specs=(columns, columns),
        check_vma=False,
    )
```

```python
import functools

import jax
import jax.numpy as jnp
from jax import lax
from jax.experimental import pallas as pl
from jax.experimental.pallas import tpu as pltpu
from jax.sharding import PartitionSpec as P

MESH = pl.DeviceIdType.MESH
VMEM_LIMIT = 56 * 1024 * 1024
BATCH = 16
DELAY = 4
CHUNKS = 4
ANY = pl.BlockSpec(memory_space=pl.ANY)
VMEM = pl.BlockSpec(memory_space=pltpu.VMEM)


def flip(index, mask):
    bit = 1
    while bit <= mask:
        if mask & bit:
            index = index + bit - 2 * bit * ((index // bit) % 2)
        bit *= 2
    return index


def bits_of(n):
    bits = []
    while 2 ** len(bits) < n:
        bits.append(2 ** len(bits))
    return bits


def spread_orders(n):
    bits = bits_of(n)
    return [bits[1:] + bits[:1], bits[:0:-1] + bits[:1]] * (CHUNKS // 2)


def sum_orders(n):
    bits = bits_of(n)
    return [bits[:1] + bits[1:], bits[:1] + bits[:0:-1]] * (CHUNKS // 2)


def chunks_of(nbd):
    edges = [nbd * k // CHUNKS for k in range(CHUNKS + 1)]
    return [(low, high - low) for low, high in zip(edges, edges[1:])]


def greet(n, group, groups, me, along_grp):
    barrier = pltpu.get_barrier_semaphore()
    bits = bits_of(n)
    for bit in bits:
        pl.semaphore_signal(barrier, inc=1, device_id=(group, flip(me, bit)), device_id_type=MESH)
    if along_grp:
        @pl.when(group > 0)
        def _():
            pl.semaphore_signal(barrier, inc=1, device_id=(group - 1, me), device_id_type=MESH)

        @pl.when(group < groups - 1)
        def _():
            pl.semaphore_signal(barrier, inc=1, device_id=(group + 1, me), device_id_type=MESH)

        ends = jnp.minimum(group, 1) + jnp.minimum(groups - 1 - group, 1)
        pl.semaphore_wait(barrier, len(bits) + ends)
    else:
        pl.semaphore_wait(barrier, len(bits))


def spread_steps(n):
    steps = []
    for chunk, order in enumerate(spread_orders(n)):
        place = {bit: k for k, bit in enumerate(order)}
        for r in range(n):
            held = [place[bit] for bit in order if r & bit]
            last = max(held) if held else -1
            steps.append((len(held), chunk, r, order[last + 1:]))
    return [step[1:] for step in sorted(steps, key=lambda s: (s[0], s[2], s[1]))]


def spread_copy(n, nbd, group, me, own, out, base, send, recv, chunk, r, bit):
    start, size = chunks_of(nbd)[chunk]
    at = pl.ds(base + flip(me, r) * nbd + start, size)
    source = own.at[pl.ds(start, size)] if r == 0 else out.at[at]
    return pltpu.make_async_remote_copy(
        src_ref=source, dst_ref=out.at[at],
        send_sem=send.at[chunk, r | bit], recv_sem=recv.at[chunk, r | bit],
        device_id=(group, flip(me, bit)), device_id_type=MESH)


def spread_here(args, chunk, r):
    if r:
        last = [bit for bit in spread_orders(args[0])[chunk] if r & bit][-1]
        spread_copy(*args, chunk, r - last, last).wait_recv()


def spread_own(args, chunks):
    orders = spread_orders(args[0])
    for k in range(len(orders[0])):
        for chunk in chunks:
            spread_copy(*args, chunk, 0, orders[chunk][k]).start()


def spread_level(args, level):
    for chunk, r, sends in spread_steps(args[0]):
        if bin(r).count("1") == level and sends:
            spread_here(args, chunk, r)
            for bit in sends:
                spread_copy(*args, chunk, r, bit).start()


def spread_ends(args):
    for chunk, r, sends in spread_steps(args[0]):
        if r and not sends:
            spread_here(args, chunk, r)


def spread_finish(n, nbd, group, me, own, out, base, send, recv):
    copy = functools.partial(spread_copy, n, nbd, group, me, own, out, base, send, recv)
    for chunk, r, sends in spread_steps(n):
        for bit in sends:
            copy(chunk, r, bit).wait_send()


def gather_kernel(n, groups, panel, out, mine, zrecv, send, recv, psend, precv, zsem, lsem):
    group, me = lax.axis_index("grp"), lax.axis_index("narrow")
    nbd = mine.shape[0]
    nbg = n * nbd
    for j in range(nbd):
        mine[j] = panel[:, j * 128:(j + 1) * 128]
    greet(n, group, groups, me, True)

    def zcopy():
        return pltpu.make_async_remote_copy(
            src_ref=mine, dst_ref=zrecv, send_sem=zsem.at[0], recv_sem=zsem.at[1],
            device_id=(group + 1, me), device_id_type=MESH)

    @pl.when(group < groups - 1)
    def _():
        zcopy().start()

    levels = range(1, len(bits_of(n)))
    keep = pltpu.make_async_copy(mine, out.at[pl.ds(nbg + me * nbd, nbd)], lsem.at[0])
    keep.start()
    own_args = (n, nbd, group, me, mine, out, nbg, send, recv)
    prior_args = (n, nbd, group, me, zrecv, out, 0, psend, precv)
    spread_own(own_args, range(CHUNKS))
    spread_level(own_args, 1)

    @pl.when(group > 0)
    def _():
        pltpu.make_async_remote_copy(
            src_ref=mine, dst_ref=zrecv, send_sem=zsem.at[0], recv_sem=zsem.at[1],
            device_id=(group - 1, me), device_id_type=MESH).wait_recv()
        kept = pltpu.make_async_copy(zrecv, out.at[pl.ds(me * nbd, nbd)], lsem.at[1])
        kept.start()
        spread_own(prior_args, range(CHUNKS))
        kept.wait()

    for level in levels:
        if level > 1:
            spread_level(own_args, level)

        @pl.when(group > 0)
        def _():
            spread_level(prior_args, level)

    spread_ends(own_args)

    @pl.when(group > 0)
    def _():
        spread_ends(prior_args)
        spread_finish(*prior_args)

    spread_finish(*own_args)
    keep.wait()

    @pl.when(group < groups - 1)
    def _():
        zcopy().wait_send()


def gather(n, groups, nbd, panel):
    cols = panel.shape[0]
    nbg = n * nbd
    return pl.pallas_call(
        functools.partial(gather_kernel, n, groups),
        out_shape=jax.ShapeDtypeStruct((2 * nbg, cols, 128), jnp.bfloat16),
        in_specs=[VMEM],
        out_specs=ANY,
        scratch_shapes=[
            pltpu.VMEM((nbd, cols, 128), jnp.bfloat16),
            pltpu.VMEM((nbd, cols, 128), jnp.bfloat16),
            pltpu.SemaphoreType.DMA((CHUNKS, n)),
            pltpu.SemaphoreType.DMA((CHUNKS, n)),
            pltpu.SemaphoreType.DMA((CHUNKS, n)),
            pltpu.SemaphoreType.DMA((CHUNKS, n)),
            pltpu.SemaphoreType.DMA((2,)),
            pltpu.SemaphoreType.DMA((2,)),
        ],
        compiler_params=pltpu.CompilerParams(
            collective_id=1, has_side_effects=True, vmem_limit_bytes=VMEM_LIMIT),
        name="gather_panel",
    )(panel)


def apply_kernel(forward, block, nbg, rows, cols, count, src, tiles, *rest):
    if forward:
        out, acc = rest
    else:
        out, filtered, acc = rest
    step = pl.program_id(0)
    live = count[0]
    group = lax.axis_index("grp")
    row0, col0 = group * nbg, (group - 1) * nbg
    nout = out.shape[0]

    @pl.when(step == 0)
    def _():
        acc[...] = jnp.zeros_like(acc)
        if not forward:
            nbd = filtered.shape[1] // 128
            first_own = lax.axis_index("narrow") * nbd
            for j in range(nbd):
                filtered[:, j * 128:(j + 1) * 128] = src[first_own + j]

    first = step * block
    here = jnp.clip(live - first, 0, block)

    def batch(b, carry):
        waiting = []

        def add():
            place, prod = waiting.pop(0)
            acc[place] += prod

        for u in range(BATCH):
            at = b * BATCH + u
            slot = first + at
            row, col = rows[slot] - row0, cols[slot] - col0
            source, place = (col, row) if forward else (row, col)
            prod = lax.dot_general(
                src[source], tiles[at], (((1,), (1 if forward else 0,)), ((), ())),
                preferred_element_type=jnp.float32)
            waiting.append((jnp.where(slot < live, place, nout), prod))
            if len(waiting) > DELAY:
                add()
        while waiting:
            add()
        return carry

    lax.fori_loop(0, (here + BATCH - 1) // BATCH, batch, 0)

    @pl.when(step == pl.num_programs(0) - 1)
    def _():
        def put(j, carry):
            out[j] = acc[j].astype(out.dtype)
            return carry
        lax.fori_loop(0, nout, put, 0, unroll=8)


def apply_tiles(forward, nbg, nbd, src, tiles, tile_row, tile_col, tile_count):
    slots, tile = tiles.shape[:2]
    kcols = src.shape[1]
    block = min(64, slots)
    nin, nout = (2 * nbg, nbg) if forward else (nbg, 2 * nbg)
    whole = lambda i, r, c, n: (0, 0, 0)
    sums = jax.ShapeDtypeStruct((nout, kcols, tile), jnp.bfloat16)
    sums_spec = pl.BlockSpec((nout, kcols, tile), whole)
    own = jax.ShapeDtypeStruct((kcols, nbd * tile), jnp.bfloat16)
    own_spec = pl.BlockSpec((kcols, nbd * tile), lambda i, r, c, n: (0, 0))
    return pl.pallas_call(
        functools.partial(apply_kernel, forward, block, nbg),
        out_shape=sums if forward else (sums, own),
        grid_spec=pltpu.PrefetchScalarGridSpec(
            num_scalar_prefetch=3,
            grid=(slots // block,),
            in_specs=[
                pl.BlockSpec((nin, kcols, tile), whole),
                pl.BlockSpec(
                    (block, tile, tile),
                    lambda i, r, c, n: (jnp.minimum(i, jnp.maximum(n[0] - 1, 0) // block), 0, 0)),
            ],
            out_specs=sums_spec if forward else (sums_spec, own_spec),
            scratch_shapes=[pltpu.VMEM((nout + 1, kcols, tile), jnp.float32)],
        ),
        compiler_params=pltpu.CompilerParams(
            dimension_semantics=("arbitrary",), vmem_limit_bytes=VMEM_LIMIT),
        name="apply_forward" if forward else "apply_transposed",
    )(tile_row, tile_col, tile_count, src, tiles)


class Summed:
    def __init__(self, n, nbd, group, me, part, base, staged, landed, send, recv):
        self.n, self.nbd, self.group, self.me = n, nbd, group, me
        self.part, self.base = part, base
        self.staged, self.landed, self.send, self.recv = staged, landed, send, recv
        self.orders = sum_orders(n)

    def copy(self, chunk, r):
        order = self.orders[chunk]
        bit = [b for b in order if r & b][0]
        start, size = chunks_of(self.nbd)[chunk]
        if bit == order[0]:
            source = self.part.at[pl.ds(self.base + flip(self.me, r) * self.nbd + start, size)]
        else:
            source = self.staged.at[r, pl.ds(start, size)]
        return pltpu.make_async_remote_copy(
            src_ref=source, dst_ref=self.landed.at[r, pl.ds(start, size)],
            send_sem=self.send.at[chunk, r], recv_sem=self.recv.at[chunk, r],
            device_id=(self.group, flip(self.me, bit)), device_id_type=MESH)

    def sent_at(self, chunk, stage):
        order = self.orders[chunk]
        done = sum(order[:stage])
        rest = [r for r in range(self.n) if r & order[stage] and not r & done]

        def needed(r):
            later = [k for k, b in enumerate(order) if r & b and k > stage]
            return later[0] if later else len(order)

        return sorted(rest, key=needed)

    def value(self, chunk, r, stage, put):
        order = self.orders[chunk]
        start, size = chunks_of(self.nbd)[chunk]
        for bit in order[:stage]:
            self.copy(chunk, r | bit).wait_recv()
        first = self.base + flip(self.me, r) * self.nbd
        for j in range(start, start + size):
            total = self.part[first + j].astype(jnp.float32)
            for bit in order[:stage]:
                total = total + self.landed[r | bit, j].astype(jnp.float32)
            put(j, total)

    def stage(self, stage):
        for chunk in range(CHUNKS):
            for r in self.sent_at(chunk, stage):
                if stage:
                    def put(j, total, r=r):
                        self.staged[r, j] = total.astype(jnp.bfloat16)
                    self.value(chunk, r, stage, put)
                self.copy(chunk, r).start()

    def finish(self, chunk, put):
        self.value(chunk, 0, len(self.orders[chunk]), put)

    def drain(self):
        for chunk in range(CHUNKS):
            for r in range(1, self.n):
                self.copy(chunk, r).wait_send()


def reduce_kernel(n, groups, part, out, mine, staged, landed, send, recv, gsend, grecv, lsem):
    group, me = lax.axis_index("grp"), lax.axis_index("narrow")
    nbd = mine.shape[0]
    greet(n, group, groups, me, False)
    summed = Summed(n, nbd, group, me, part, 0, staged, landed, send, recv)
    for stage in range(len(bits_of(n))):
        summed.stage(stage)

    def put(j, total):
        mine[j] = total.astype(jnp.bfloat16)

    args = (n, nbd, group, me, mine, out, 0, gsend, grecv)
    for pair in range(0, CHUNKS, 2):
        for chunk in (pair, pair + 1):
            summed.finish(chunk, put)
        spread_own(args, (pair, pair + 1))
    keep = pltpu.make_async_copy(mine, out.at[pl.ds(me * nbd, nbd)], lsem.at[0])
    keep.start()
    for level in range(1, len(bits_of(n))):
        spread_level(args, level)
    spread_ends(args)
    summed.drain()
    spread_finish(*args)
    keep.wait()


def reduce_rows(n, groups, nbd, part):
    nbg, cols = part.shape[:2]
    return pl.pallas_call(
        functools.partial(reduce_kernel, n, groups),
        out_shape=jax.ShapeDtypeStruct((nbg, cols, 128), jnp.bfloat16),
        in_specs=[VMEM],
        out_specs=ANY,
        scratch_shapes=[
            pltpu.VMEM((nbd, cols, 128), jnp.bfloat16),
            pltpu.VMEM((n, nbd, cols, 128), jnp.bfloat16),
            pltpu.VMEM((n, nbd, cols, 128), jnp.bfloat16),
            pltpu.SemaphoreType.DMA((CHUNKS, n)),
            pltpu.SemaphoreType.DMA((CHUNKS, n)),
            pltpu.SemaphoreType.DMA((CHUNKS, n)),
            pltpu.SemaphoreType.DMA((CHUNKS, n)),
            pltpu.SemaphoreType.DMA((1,)),
        ],
        compiler_params=pltpu.CompilerParams(
            collective_id=2, has_side_effects=True, vmem_limit_bytes=VMEM_LIMIT),
        name="reduce_rows",
    )(part)


def image_kernel(n, groups, part, out, mine, zrecv, pstaged, planded, ostaged, olanded,
                 psend, precv, osend, orecv, zsem):
    group, me = lax.axis_index("grp"), lax.axis_index("narrow")
    nbd = mine.shape[0]
    greet(n, group, groups, me, True)
    prior = Summed(n, nbd, group, me, part, 0, pstaged, planded, psend, precv)
    own = Summed(n, nbd, group, me, part, n * nbd, ostaged, olanded, osend, orecv)

    def zcopy(target):
        return pltpu.make_async_remote_copy(
            src_ref=mine, dst_ref=zrecv, send_sem=zsem.at[0], recv_sem=zsem.at[1],
            device_id=(target, me), device_id_type=MESH)

    for stage in range(len(bits_of(n))):
        @pl.when(group > 0)
        def _():
            prior.stage(stage)
        own.stage(stage)

    @pl.when(group > 0)
    def _():
        def put(j, total):
            mine[j] = total.astype(jnp.bfloat16)
        for chunk in range(CHUNKS):
            prior.finish(chunk, put)
        zcopy(group - 1).start()

    def put_own(j, total):
        out[:, j * 128:(j + 1) * 128] = total

    for chunk in range(CHUNKS):
        own.finish(chunk, put_own)

    @pl.when(group < groups - 1)
    def _():
        zcopy(group + 1).wait_recv()
        for j in range(nbd):
            at = slice(j * 128, (j + 1) * 128)
            out[:, at] = out[:, at] + zrecv[j].astype(jnp.float32)

    own.drain()

    @pl.when(group > 0)
    def _():
        prior.drain()
        zcopy(group - 1).wait_send()


def image(n, groups, nbd, part):
    cols = part.shape[1]
    held = pltpu.VMEM((n, nbd, cols, 128), jnp.bfloat16)
    sems = pltpu.SemaphoreType.DMA((CHUNKS, n))
    piece = pltpu.VMEM((nbd, cols, 128), jnp.bfloat16)
    return pl.pallas_call(
        functools.partial(image_kernel, n, groups),
        out_shape=jax.ShapeDtypeStruct((cols, nbd * 128), jnp.float32),
        in_specs=[VMEM],
        out_specs=VMEM,
        scratch_shapes=[piece, piece, held, held, held, held, sems, sems, sems, sems,
                        pltpu.SemaphoreType.DMA((2,))],
        compiler_params=pltpu.CompilerParams(
            collective_id=3, has_side_effects=True, vmem_limit_bytes=VMEM_LIMIT),
        name="image_sums",
    )(part)


def body(panel, tiles, tile_row, tile_col, tile_count):
    tile = tiles.shape[1]
    nbd = panel.shape[1] // tile
    n, groups = lax.axis_size("narrow"), lax.axis_size("grp")
    nbg = nbd * n
    both = gather(n, groups, nbd, panel)
    part = apply_tiles(True, nbg, nbd, both, tiles, tile_row, tile_col, tile_count)
    rows = reduce_rows(n, groups, nbd, part)
    sums, filtered = apply_tiles(False, nbg, nbd, rows, tiles, tile_row, tile_col, tile_count)
    return filtered, image(n, groups, nbd, sums)


def solution(mesh):
    spread = P(("grp", "narrow"))
    columns = P(None, ("grp", "narrow"))
    return jax.shard_map(
        body,
        mesh=mesh,
        in_specs=(columns, P(("grp", "narrow"), None, None), spread, spread, spread),
        out_specs=(columns, columns),
        check_vma=False,
    )
```

```python
import functools

import jax
import jax.numpy as jnp
from jax import lax
from jax.experimental import pallas as pl
from jax.experimental.pallas import tpu as pltpu
from jax.sharding import PartitionSpec as P

MESH = pl.DeviceIdType.MESH
VMEM_LIMIT = 56 * 1024 * 1024
BATCH = 32
DELAY = 4
CHUNKS = 4
PLAIN, ALONG = (0, 1), (2, 3)
ANY = pl.BlockSpec(memory_space=pl.ANY)
VMEM = pl.BlockSpec(memory_space=pltpu.VMEM)


def flip(index, mask):
    bit = 1
    while bit <= mask:
        if mask & bit:
            index = index + bit - 2 * bit * ((index // bit) % 2)
        bit *= 2
    return index


def bits_of(n):
    bits = []
    while 2 ** len(bits) < n:
        bits.append(2 ** len(bits))
    return bits


def spread_orders(n):
    bits = bits_of(n)
    return [bits[1:] + bits[:1], bits[:0:-1] + bits[:1]] * (CHUNKS // 2)


def sum_orders(n):
    bits = bits_of(n)
    return [bits[:1] + bits[1:], bits[:1] + bits[:0:-1]] * (CHUNKS // 2)


def chunks_of(nbd):
    big = -(-nbd // CHUNKS)
    edges = [0, big, 2 * big, 2 * big + (nbd - 2 * big) // 2, nbd]
    return [(low, high - low) for low, high in zip(edges, edges[1:])]


def greet(n, group, groups, me, along_grp):
    barrier = pltpu.get_barrier_semaphore()
    bits = bits_of(n)
    for bit in bits:
        pl.semaphore_signal(barrier, inc=1, device_id=(group, flip(me, bit)), device_id_type=MESH)
    if along_grp:
        @pl.when(group > 0)
        def _():
            pl.semaphore_signal(barrier, inc=1, device_id=(group - 1, me), device_id_type=MESH)

        @pl.when(group < groups - 1)
        def _():
            pl.semaphore_signal(barrier, inc=1, device_id=(group + 1, me), device_id_type=MESH)

        ends = jnp.minimum(group, 1) + jnp.minimum(groups - 1 - group, 1)
        pl.semaphore_wait(barrier, len(bits) + ends)
    else:
        pl.semaphore_wait(barrier, len(bits))


def spread_steps(n):
    steps = []
    for chunk, order in enumerate(spread_orders(n)):
        place = {bit: k for k, bit in enumerate(order)}
        for r in range(n):
            held = [place[bit] for bit in order if r & bit]
            last = max(held) if held else -1
            steps.append((len(held), chunk, r, order[last + 1:]))
    return [step[1:] for step in sorted(steps, key=lambda s: (s[0], s[2], s[1]))]


def spread_copy(n, nbd, group, me, own, out, base, send, recv, chunk, r, bit):
    start, size = chunks_of(nbd)[chunk]
    at = pl.ds(base + flip(me, r) * nbd + start, size)
    source = out.at[at] if r or own is None else own.at[pl.ds(start, size)]
    return pltpu.make_async_remote_copy(
        src_ref=source, dst_ref=out.at[at],
        send_sem=send.at[chunk, r | bit], recv_sem=recv.at[chunk, r | bit],
        device_id=(group, flip(me, bit)), device_id_type=MESH)


def spread_here(args, chunk, r):
    if r:
        last = [bit for bit in spread_orders(args[0])[chunk] if r & bit][-1]
        spread_copy(*args, chunk, r - last, last).wait_recv()


def spread_own(args, chunks):
    orders = spread_orders(args[0])
    for k in range(len(orders[0])):
        for chunk in chunks:
            spread_copy(*args, chunk, 0, orders[chunk][k]).start()


def spread_level(args, level, chunks, also=None):
    for chunk, r, sends in spread_steps(args[0]):
        if chunk in chunks and bin(r).count("1") == level and sends:
            spread_here(args, chunk, r)
            for bit in sends:
                spread_copy(*args, chunk, r, bit).start()
            if also is not None:
                also(chunk, r)


def spread_ends(args, chunks):
    for chunk, r, sends in spread_steps(args[0]):
        if chunk in chunks and r and not sends:
            spread_here(args, chunk, r)


def spread_finish(n, nbd, group, me, own, out, base, send, recv, chunks):
    copy = functools.partial(spread_copy, n, nbd, group, me, own, out, base, send, recv)
    for chunk, r, sends in spread_steps(n):
        for bit in sends if chunk in chunks else ():
            copy(chunk, r, bit).wait_send()


def gather_kernel(n, groups, panel, out, mine, send, recv, psend, precv, zsend, zrecv, lsem):
    group, me = lax.axis_index("grp"), lax.axis_index("narrow")
    nbd = mine.shape[0]
    nbg = n * nbd
    levels = len(bits_of(n))
    every = range(CHUNKS)
    evens = sorted(range(0, n, 2), key=lambda r: bin(r).count("1"))
    for j in range(nbd):
        mine[j] = panel[:, j * 128:(j + 1) * 128]
    greet(n, group, groups, me, True)

    def zcopy(chunk, r, target):
        start, size = chunks_of(nbd)[chunk]
        at = flip(me, r) * nbd + start
        source = out.at[pl.ds(nbg + at, size)] if r else mine.at[pl.ds(start, size)]
        return pltpu.make_async_remote_copy(
            src_ref=source, dst_ref=out.at[pl.ds(at, size)],
            send_sem=zsend.at[chunk, r], recv_sem=zrecv.at[chunk, r],
            device_id=(target, me), device_id_type=MESH)

    own = (n, nbd, group, me, mine, out, nbg, send, recv)
    prior = (n, nbd, group, me, None, out, 0, psend, precv)

    @pl.when(group < groups - 1)
    def _():
        for chunk in every:
            zcopy(chunk, 0, group + 1).start()

    spread_own(own, every)
    keep = pltpu.make_async_copy(mine, out.at[pl.ds(nbg + me * nbd, nbd)], lsem.at[0])
    keep.start()

    def up(chunk, r):
        if chunk in ALONG and r % 2 == 0:
            @pl.when(group < groups - 1)
            def _():
                zcopy(chunk, r, group + 1).start()

    for level in range(1, levels):
        spread_level(own, level, every, up)

        @pl.when(group > 0)
        def _():
            if level == 1:
                for chunk in PLAIN:
                    zcopy(chunk, 0, group - 1).wait_recv()
                spread_own(prior, PLAIN)
            for r in evens:
                if bin(r).count("1") == level - 1:
                    for chunk in ALONG:
                        zcopy(chunk, r, group - 1).wait_recv()
                        spread_copy(*prior, chunk, r, 1).start()

    @pl.when(group > 0)
    def _():
        for level in range(1, levels):
            spread_level(prior, level, PLAIN)
        for r in evens:
            if bin(r).count("1") >= levels - 1:
                for chunk in ALONG:
                    zcopy(chunk, r, group - 1).wait_recv()
                    spread_copy(*prior, chunk, r, 1).start()

    spread_ends(own, every)

    @pl.when(group > 0)
    def _():
        spread_ends(prior, PLAIN)
        spread_finish(*prior, PLAIN)
        for chunk in ALONG:
            for r in evens:
                spread_copy(*prior, chunk, r, 1).wait()

    spread_finish(*own, every)
    keep.wait()

    @pl.when(group < groups - 1)
    def _():
        for chunk in every:
            for r in evens if chunk in ALONG else (0,):
                zcopy(chunk, r, group + 1).wait_send()


def gather(n, groups, nbd, panel):
    cols = panel.shape[0]
    nbg = n * nbd
    return pl.pallas_call(
        functools.partial(gather_kernel, n, groups),
        out_shape=jax.ShapeDtypeStruct((2 * nbg, cols, 128), jnp.bfloat16),
        in_specs=[VMEM],
        out_specs=ANY,
        scratch_shapes=[
            pltpu.VMEM((nbd, cols, 128), jnp.bfloat16),
            pltpu.SemaphoreType.DMA((CHUNKS, n)),
            pltpu.SemaphoreType.DMA((CHUNKS, n)),
            pltpu.SemaphoreType.DMA((CHUNKS, n)),
            pltpu.SemaphoreType.DMA((CHUNKS, n)),
            pltpu.SemaphoreType.DMA((CHUNKS, n)),
            pltpu.SemaphoreType.DMA((CHUNKS, n)),
            pltpu.SemaphoreType.DMA((1,)),
        ],
        compiler_params=pltpu.CompilerParams(
            collective_id=1, has_side_effects=True, vmem_limit_bytes=VMEM_LIMIT),
        name="gather_panel",
    )(panel)


def apply_kernel(forward, block, nbg, rows, cols, count, src, tiles, *rest):
    if forward:
        out, acc = rest
    else:
        out, filtered, acc = rest
    step = pl.program_id(0)
    live = count[0]
    group = lax.axis_index("grp")
    row0, col0 = group * nbg, (group - 1) * nbg
    nout = out.shape[0]

    @pl.when(step == 0)
    def _():
        acc[...] = jnp.zeros_like(acc)
        if not forward:
            nbd = filtered.shape[1] // 128
            first_own = lax.axis_index("narrow") * nbd
            for j in range(nbd):
                filtered[:, j * 128:(j + 1) * 128] = src[first_own + j]

    first = step * block
    here = jnp.clip(live - first, 0, block)

    def batch(b, carry):
        waiting = []

        def add():
            place, prod = waiting.pop(0)
            acc[place] += prod

        for u in range(BATCH):
            at = b * BATCH + u
            slot = first + at
            row, col = rows[slot] - row0, cols[slot] - col0
            source, place = (col, row) if forward else (row, col)
            prod = lax.dot_general(
                src[source], tiles[at], (((1,), (1 if forward else 0,)), ((), ())),
                preferred_element_type=jnp.float32)
            waiting.append((jnp.where(slot < live, place, nout), prod))
            if len(waiting) > DELAY:
                add()
        while waiting:
            add()
        return carry

    lax.fori_loop(0, (here + BATCH - 1) // BATCH, batch, 0)

    @pl.when(step == pl.num_programs(0) - 1)
    def _():
        def put(j, carry):
            out[j] = acc[j].astype(out.dtype)
            return carry
        lax.fori_loop(0, nout, put, 0, unroll=8)


def apply_tiles(forward, nbg, nbd, src, tiles, tile_row, tile_col, tile_count):
    slots, tile = tiles.shape[:2]
    kcols = src.shape[1]
    block = min(64, slots)
    nin, nout = (2 * nbg, nbg) if forward else (nbg, 2 * nbg)
    whole = lambda i, r, c, n: (0, 0, 0)
    sums = jax.ShapeDtypeStruct((nout, kcols, tile), jnp.bfloat16)
    sums_spec = pl.BlockSpec((nout, kcols, tile), whole)
    own = jax.ShapeDtypeStruct((kcols, nbd * tile), jnp.bfloat16)
    own_spec = pl.BlockSpec((kcols, nbd * tile), lambda i, r, c, n: (0, 0))
    return pl.pallas_call(
        functools.partial(apply_kernel, forward, block, nbg),
        out_shape=sums if forward else (sums, own),
        grid_spec=pltpu.PrefetchScalarGridSpec(
            num_scalar_prefetch=3,
            grid=(slots // block,),
            in_specs=[
                pl.BlockSpec((nin, kcols, tile), whole),
                pl.BlockSpec(
                    (block, tile, tile),
                    lambda i, r, c, n: (jnp.minimum(i, jnp.maximum(n[0] - 1, 0) // block), 0, 0)),
            ],
            out_specs=sums_spec if forward else (sums_spec, own_spec),
            scratch_shapes=[pltpu.VMEM((nout + 1, kcols, tile), jnp.float32)],
        ),
        compiler_params=pltpu.CompilerParams(
            dimension_semantics=("arbitrary",), vmem_limit_bytes=VMEM_LIMIT),
        name="apply_forward" if forward else "apply_transposed",
    )(tile_row, tile_col, tile_count, src, tiles)


class Summed:
    def __init__(self, n, nbd, group, me, part, base, local, lsem, staged, landed, send, recv):
        self.n, self.nbd, self.group, self.me = n, nbd, group, me
        self.part, self.base, self.local, self.lsem = part, base, local, lsem
        self.staged, self.landed, self.send, self.recv = staged, landed, send, recv
        self.orders = sum_orders(n)

    def fetch(self, r):
        at = pl.ds(self.base + flip(self.me, r) * self.nbd, self.nbd)
        return pltpu.make_async_copy(self.part.at[at], self.local.at[r // 2], self.lsem.at[r // 2])

    def begin(self):
        for r in range(0, self.n, 2):
            self.fetch(r).start()

    def fetched(self):
        for r in range(0, self.n, 2):
            self.fetch(r).wait()

    def copy(self, chunk, r):
        order = self.orders[chunk]
        bit = [b for b in order if r & b][0]
        start, size = chunks_of(self.nbd)[chunk]
        if bit == order[0]:
            source = self.part.at[pl.ds(self.base + flip(self.me, r) * self.nbd + start, size)]
        else:
            source = self.staged.at[r, pl.ds(start, size)]
        return pltpu.make_async_remote_copy(
            src_ref=source, dst_ref=self.landed.at[r, pl.ds(start, size)],
            send_sem=self.send.at[chunk, r], recv_sem=self.recv.at[chunk, r],
            device_id=(self.group, flip(self.me, bit)), device_id_type=MESH)

    def sent_at(self, chunk, stage):
        order = self.orders[chunk]
        done = sum(order[:stage])
        rest = [r for r in range(self.n) if r & order[stage] and not r & done]

        def needed(r):
            later = [k for k, b in enumerate(order) if r & b and k > stage]
            return later[0] if later else len(order)

        return sorted(rest, key=needed)

    def value(self, chunk, r, stage, put, more=None):
        order = self.orders[chunk]
        start, size = chunks_of(self.nbd)[chunk]
        for bit in order[:stage]:
            self.copy(chunk, r | bit).wait_recv()
        for j in range(start, start + size):
            total = self.local[r // 2, j].astype(jnp.float32)
            for bit in order[:stage]:
                total = total + self.landed[r | bit, j].astype(jnp.float32)
            if more is not None:
                total = total + more[r // 2, j].astype(jnp.float32)
            put(j, total)

    def stage(self, stage, chunks, ready=None, more=None):
        for chunk in chunks:
            for r in self.sent_at(chunk, stage):
                if stage:
                    def put(j, total, r=r):
                        self.staged[r, j] = total.astype(jnp.bfloat16)
                    if ready is not None:
                        ready(chunk, r)
                    self.value(chunk, r, stage, put, more)
                self.copy(chunk, r).start()

    def finish(self, chunk, put, more=None):
        self.value(chunk, 0, len(self.orders[chunk]), put, more)

    def drain(self, first_stage_only=()):
        for chunk in range(CHUNKS):
            for r in range(1, self.n):
                if chunk not in first_stage_only or r & self.orders[chunk][0]:
                    self.copy(chunk, r).wait_send()


def reduce_kernel(n, groups, part, out, mine, local, psem, staged, landed, send, recv, gsend, grecv, lsem):
    group, me = lax.axis_index("grp"), lax.axis_index("narrow")
    nbd = mine.shape[0]
    greet(n, group, groups, me, False)
    summed = Summed(n, nbd, group, me, part, 0, local, psem, staged, landed, send, recv)
    every = range(CHUNKS)
    summed.stage(0, every)
    summed.begin()
    summed.fetched()
    for stage in range(1, len(bits_of(n))):
        summed.stage(stage, every)

    def put(j, total):
        mine[j] = total.astype(jnp.bfloat16)

    args = (n, nbd, group, me, mine, out, 0, gsend, grecv)
    for pair in range(0, CHUNKS, 2):
        for chunk in (pair, pair + 1):
            summed.finish(chunk, put)
        spread_own(args, (pair, pair + 1))
    keep = pltpu.make_async_copy(mine, out.at[pl.ds(me * nbd, nbd)], lsem.at[0])
    keep.start()
    for level in range(1, len(bits_of(n))):
        spread_level(args, level, every)
    spread_ends(args, every)
    summed.drain()
    spread_finish(*args, every)
    keep.wait()


def reduce_rows(n, groups, nbd, part):
    nbg, cols = part.shape[:2]
    return pl.pallas_call(
        functools.partial(reduce_kernel, n, groups),
        out_shape=jax.ShapeDtypeStruct((nbg, cols, 128), jnp.bfloat16),
        in_specs=[ANY],
        out_specs=ANY,
        scratch_shapes=[
            pltpu.VMEM((nbd, cols, 128), jnp.bfloat16),
            pltpu.VMEM((n // 2, nbd, cols, 128), jnp.bfloat16),
            pltpu.SemaphoreType.DMA((n // 2,)),
            pltpu.VMEM((n, nbd, cols, 128), jnp.bfloat16),
            pltpu.VMEM((n, nbd, cols, 128), jnp.bfloat16),
            pltpu.SemaphoreType.DMA((CHUNKS, n)),
            pltpu.SemaphoreType.DMA((CHUNKS, n)),
            pltpu.SemaphoreType.DMA((CHUNKS, n)),
            pltpu.SemaphoreType.DMA((CHUNKS, n)),
            pltpu.SemaphoreType.DMA((1,)),
        ],
        compiler_params=pltpu.CompilerParams(
            collective_id=2, has_side_effects=True, vmem_limit_bytes=VMEM_LIMIT),
        name="reduce_rows",
    )(part)


def image_kernel(n, groups, part, out, plocal, olocal, pfetch, ofetch, pstaged, planded, ostaged, olanded,
                 psend, precv, osend, orecv, zstaged, zlanded, zsend, zrecv):
    group, me = lax.axis_index("grp"), lax.axis_index("narrow")
    nbd = zstaged.shape[1]
    stages = len(bits_of(n))
    greet(n, group, groups, me, True)
    prior = Summed(n, nbd, group, me, part, 0, plocal, pfetch, pstaged, planded, psend, precv)
    own = Summed(n, nbd, group, me, part, n * nbd, olocal, ofetch, ostaged, olanded, osend, orecv)

    def zcopy(chunk, r, target):
        at = pl.ds(*chunks_of(nbd)[chunk])
        return pltpu.make_async_remote_copy(
            src_ref=zstaged.at[r // 2, at], dst_ref=zlanded.at[r // 2, at],
            send_sem=zsend.at[chunk, r], recv_sem=zrecv.at[chunk, r],
            device_id=(target, me), device_id_type=MESH)

    def down(chunk, r, stage):
        def put(j, total):
            zstaged[r // 2, j] = total.astype(jnp.bfloat16)
        prior.value(chunk, r, stage, put)
        zcopy(chunk, r, group - 1).start()

    def ready(chunk, r):
        @pl.when(group < groups - 1)
        def _():
            zcopy(chunk, r, group + 1).wait_recv()

    @pl.when(group > 0)
    def _():
        prior.stage(0, ALONG + PLAIN)
        prior.begin()

    own.stage(0, PLAIN + ALONG)
    own.begin()

    @pl.when(group == groups - 1)
    def _():
        zlanded[...] = jnp.zeros_like(zlanded)

    @pl.when(group > 0)
    def _():
        prior.fetched()
        for r in sorted(range(0, n, 2), reverse=True):
            for chunk in ALONG:
                down(chunk, r, 1)
        prior.stage(1, PLAIN)

    own.fetched()
    own.stage(1, PLAIN)
    for stage in range(2, stages):
        @pl.when(group > 0)
        def _():
            prior.stage(stage, PLAIN)
    own.stage(1, ALONG, ready, zlanded)

    @pl.when(group > 0)
    def _():
        for chunk in PLAIN:
            down(chunk, 0, stages)

    for stage in range(2, stages):
        own.stage(stage, PLAIN)
        own.stage(stage, ALONG, ready, zlanded)

    def put_own(j, total):
        out[:, j * 128:(j + 1) * 128] = total

    for chunk in ALONG + PLAIN:
        ready(chunk, 0)
        own.finish(chunk, put_own, zlanded)

    own.drain()

    @pl.when(group > 0)
    def _():
        prior.drain(ALONG)
        for chunk in range(CHUNKS):
            for r in range(0, n, 2) if chunk in ALONG else (0,):
                zcopy(chunk, r, group - 1).wait_send()


def image(n, groups, nbd, part):
    cols = part.shape[1]
    held = pltpu.VMEM((n, nbd, cols, 128), jnp.bfloat16)
    evens = pltpu.VMEM((n // 2, nbd, cols, 128), jnp.bfloat16)
    fetch = pltpu.SemaphoreType.DMA((n // 2,))
    sems = pltpu.SemaphoreType.DMA((CHUNKS, n))
    return pl.pallas_call(
        functools.partial(image_kernel, n, groups),
        out_shape=jax.ShapeDtypeStruct((cols, nbd * 128), jnp.float32),
        in_specs=[ANY],
        out_specs=VMEM,
        scratch_shapes=[evens, evens, fetch, fetch, held, held, held, held, sems, sems, sems, sems,
                        evens, evens, sems, sems],
        compiler_params=pltpu.CompilerParams(
            collective_id=3, has_side_effects=True, vmem_limit_bytes=VMEM_LIMIT),
        name="image_sums",
    )(part)


def body(panel, tiles, tile_row, tile_col, tile_count):
    tile = tiles.shape[1]
    nbd = panel.shape[1] // tile
    n, groups = lax.axis_size("narrow"), lax.axis_size("grp")
    nbg = nbd * n
    both = gather(n, groups, nbd, panel)
    part = apply_tiles(True, nbg, nbd, both, tiles, tile_row, tile_col, tile_count)
    rows = reduce_rows(n, groups, nbd, part)
    sums, filtered = apply_tiles(False, nbg, nbd, rows, tiles, tile_row, tile_col, tile_count)
    return filtered, image(n, groups, nbd, sums)


def solution(mesh):
    spread = P(("grp", "narrow"))
    columns = P(None, ("grp", "narrow"))
    return jax.shard_map(
        body,
        mesh=mesh,
        in_specs=(columns, P(("grp", "narrow"), None, None), spread, spread, spread),
        out_specs=(columns, columns),
        check_vma=False,
    )
```

```python
import functools

import jax
import jax.numpy as jnp
from jax import lax
from jax.experimental import pallas as pl
from jax.experimental.pallas import tpu as pltpu
from jax.sharding import PartitionSpec as P

MESH = pl.DeviceIdType.MESH
VMEM_LIMIT = 56 * 1024 * 1024
BATCH = 32
DELAY = 4
CHUNKS = 4
PLAIN, ALONG = (0, 1), (2, 3)
ANY = pl.BlockSpec(memory_space=pl.ANY)
VMEM = pl.BlockSpec(memory_space=pltpu.VMEM)


def flip(index, mask):
    bit = 1
    while bit <= mask:
        if mask & bit:
            index = index + bit - 2 * bit * ((index // bit) % 2)
        bit *= 2
    return index


def bits_of(n):
    bits = []
    while 2 ** len(bits) < n:
        bits.append(2 ** len(bits))
    return bits


def spread_orders(n):
    bits = bits_of(n)
    return [bits[1:] + bits[:1], bits[:0:-1] + bits[:1]] * (CHUNKS // 2)


def sum_orders(n):
    bits = bits_of(n)
    return [bits[:1] + bits[1:], bits[:1] + bits[:0:-1]] * (CHUNKS // 2)


def chunks_of(nbd):
    big = -(-nbd // CHUNKS)
    edges = [0, big, 2 * big, 2 * big + (nbd - 2 * big) // 2, nbd]
    return [(low, high - low) for low, high in zip(edges, edges[1:])]


def greet(n, group, groups, me, along_grp):
    barrier = pltpu.get_barrier_semaphore()
    bits = bits_of(n)
    for bit in bits:
        pl.semaphore_signal(barrier, inc=1, device_id=(group, flip(me, bit)), device_id_type=MESH)
    if along_grp:
        @pl.when(group > 0)
        def _():
            pl.semaphore_signal(barrier, inc=1, device_id=(group - 1, me), device_id_type=MESH)

        @pl.when(group < groups - 1)
        def _():
            pl.semaphore_signal(barrier, inc=1, device_id=(group + 1, me), device_id_type=MESH)

        ends = jnp.minimum(group, 1) + jnp.minimum(groups - 1 - group, 1)
        pl.semaphore_wait(barrier, len(bits) + ends)
    else:
        pl.semaphore_wait(barrier, len(bits))


def spread_steps(n):
    steps = []
    for chunk, order in enumerate(spread_orders(n)):
        place = {bit: k for k, bit in enumerate(order)}
        for r in range(n):
            held = [place[bit] for bit in order if r & bit]
            last = max(held) if held else -1
            steps.append((len(held), chunk, r, order[last + 1:]))
    return [step[1:] for step in sorted(steps, key=lambda s: (s[0], s[2], s[1]))]


def spread_copy(n, nbd, group, me, own, out, base, send, recv, chunk, r, bit):
    start, size = chunks_of(nbd)[chunk]
    at = pl.ds(base + flip(me, r) * nbd + start, size)
    source = out.at[at] if r or own is None else own.at[pl.ds(start, size)]
    return pltpu.make_async_remote_copy(
        src_ref=source, dst_ref=out.at[at],
        send_sem=send.at[chunk, r | bit], recv_sem=recv.at[chunk, r | bit],
        device_id=(group, flip(me, bit)), device_id_type=MESH)


def spread_here(args, chunk, r):
    if r:
        last = [bit for bit in spread_orders(args[0])[chunk] if r & bit][-1]
        spread_copy(*args, chunk, r - last, last).wait_recv()


def spread_own(args, chunks):
    orders = spread_orders(args[0])
    for k in range(len(orders[0])):
        for chunk in chunks:
            spread_copy(*args, chunk, 0, orders[chunk][k]).start()


def spread_level(args, level, chunks, also=None):
    for chunk, r, sends in spread_steps(args[0]):
        if chunk in chunks and bin(r).count("1") == level and sends:
            spread_here(args, chunk, r)
            for bit in sends:
                spread_copy(*args, chunk, r, bit).start()
            if also is not None:
                also(chunk, r)


def spread_ends(args, chunks):
    for chunk, r, sends in spread_steps(args[0]):
        if chunk in chunks and r and not sends:
            spread_here(args, chunk, r)


def spread_finish(n, nbd, group, me, own, out, base, send, recv, chunks):
    copy = functools.partial(spread_copy, n, nbd, group, me, own, out, base, send, recv)
    for chunk, r, sends in spread_steps(n):
        for bit in sends if chunk in chunks else ():
            copy(chunk, r, bit).wait_send()


def gather_kernel(n, groups, panel, out, mine, send, recv, psend, precv, zsend, zrecv, lsem):
    group, me = lax.axis_index("grp"), lax.axis_index("narrow")
    nbd = mine.shape[0]
    nbg = n * nbd
    levels = len(bits_of(n))
    every = range(CHUNKS)
    evens = sorted(range(0, n, 2), key=lambda r: bin(r).count("1"))
    for j in range(nbd):
        mine[j] = panel[:, j * 128:(j + 1) * 128]
    greet(n, group, groups, me, True)

    def zcopy(chunk, r, target):
        start, size = chunks_of(nbd)[chunk]
        at = flip(me, r) * nbd + start
        source = out.at[pl.ds(nbg + at, size)] if r else mine.at[pl.ds(start, size)]
        return pltpu.make_async_remote_copy(
            src_ref=source, dst_ref=out.at[pl.ds(at, size)],
            send_sem=zsend.at[chunk, r], recv_sem=zrecv.at[chunk, r],
            device_id=(target, me), device_id_type=MESH)

    own = (n, nbd, group, me, mine, out, nbg, send, recv)
    prior = (n, nbd, group, me, None, out, 0, psend, precv)

    @pl.when(group < groups - 1)
    def _():
        for chunk in every:
            zcopy(chunk, 0, group + 1).start()

    spread_own(own, every)
    keep = pltpu.make_async_copy(mine, out.at[pl.ds(nbg + me * nbd, nbd)], lsem.at[0])
    keep.start()

    def up(chunk, r):
        if chunk in ALONG and r % 2 == 0:
            @pl.when(group < groups - 1)
            def _():
                zcopy(chunk, r, group + 1).start()

    for level in range(1, levels):
        spread_level(own, level, every, up)

        @pl.when(group > 0)
        def _():
            if level == 1:
                for chunk in PLAIN:
                    zcopy(chunk, 0, group - 1).wait_recv()
                spread_own(prior, PLAIN)
            for r in evens:
                if bin(r).count("1") == level - 1:
                    for chunk in ALONG:
                        zcopy(chunk, r, group - 1).wait_recv()
                        spread_copy(*prior, chunk, r, 1).start()

    @pl.when(group > 0)
    def _():
        for level in range(1, levels):
            spread_level(prior, level, PLAIN)
        for r in evens:
            if bin(r).count("1") >= levels - 1:
                for chunk in ALONG:
                    zcopy(chunk, r, group - 1).wait_recv()
                    spread_copy(*prior, chunk, r, 1).start()

    spread_ends(own, every)

    @pl.when(group > 0)
    def _():
        spread_ends(prior, PLAIN)
        spread_finish(*prior, PLAIN)
        for chunk in ALONG:
            for r in evens:
                spread_copy(*prior, chunk, r, 1).wait()

    spread_finish(*own, every)
    keep.wait()

    @pl.when(group < groups - 1)
    def _():
        for chunk in every:
            for r in evens if chunk in ALONG else (0,):
                zcopy(chunk, r, group + 1).wait_send()


def gather(n, groups, nbd, panel):
    cols = panel.shape[0]
    nbg = n * nbd
    return pl.pallas_call(
        functools.partial(gather_kernel, n, groups),
        out_shape=jax.ShapeDtypeStruct((2 * nbg, cols, 128), jnp.bfloat16),
        in_specs=[VMEM],
        out_specs=VMEM,
        scratch_shapes=[
            pltpu.VMEM((nbd, cols, 128), jnp.bfloat16),
            pltpu.SemaphoreType.DMA((CHUNKS, n)),
            pltpu.SemaphoreType.DMA((CHUNKS, n)),
            pltpu.SemaphoreType.DMA((CHUNKS, n)),
            pltpu.SemaphoreType.DMA((CHUNKS, n)),
            pltpu.SemaphoreType.DMA((CHUNKS, n)),
            pltpu.SemaphoreType.DMA((CHUNKS, n)),
            pltpu.SemaphoreType.DMA((1,)),
        ],
        compiler_params=pltpu.CompilerParams(
            collective_id=1, has_side_effects=True, vmem_limit_bytes=VMEM_LIMIT),
        name="gather_panel",
    )(panel)


def apply_kernel(forward, block, nbg, rows, cols, count, source_blocks, tiles, *rest):
    if forward:
        sums, acc, src, out, fetched, sent = rest
    else:
        sums, filtered, acc, src, out, fetched, sent = rest
    step = pl.program_id(0)
    live = count[0]
    group = lax.axis_index("grp")
    row0, col0 = group * nbg, (group - 1) * nbg
    nout = out.shape[0]

    @pl.when(step == 0)
    def _():
        fetch = pltpu.make_async_copy(source_blocks, src, fetched.at[0])
        fetch.start()
        acc[...] = jnp.zeros_like(acc)
        fetch.wait()
        if not forward:
            nbd = filtered.shape[1] // 128
            first_own = lax.axis_index("narrow") * nbd
            for j in range(nbd):
                filtered[:, j * 128:(j + 1) * 128] = src[first_own + j]

    first = step * block
    here = jnp.clip(live - first, 0, block)

    def batch(b, carry):
        waiting = []

        def add():
            place, prod = waiting.pop(0)
            acc[place] += prod

        for u in range(BATCH):
            at = b * BATCH + u
            slot = first + at
            row, col = rows[slot] - row0, cols[slot] - col0
            source, place = (col, row) if forward else (row, col)
            prod = lax.dot_general(
                src[source], tiles[at], (((1,), (1 if forward else 0,)), ((), ())),
                preferred_element_type=jnp.float32)
            waiting.append((jnp.where(slot < live, place, nout), prod))
            if len(waiting) > DELAY:
                add()
        while waiting:
            add()
        return carry

    lax.fori_loop(0, (here + BATCH - 1) // BATCH, batch, 0)

    @pl.when(step == pl.num_programs(0) - 1)
    def _():
        parts = sent.shape[0]
        size = nout // parts
        for k in range(parts):
            def put(j, carry):
                out[j] = acc[j].astype(out.dtype)
                return carry
            lax.fori_loop(k * size, (k + 1) * size, put, 0, unroll=4)
            at = pl.ds(k * size, size)
            pltpu.make_async_copy(out.at[at], sums.at[at], sent.at[k]).start()
        for k in range(parts):
            at = pl.ds(k * size, size)
            pltpu.make_async_copy(out.at[at], sums.at[at], sent.at[k]).wait()


def apply_tiles(forward, nbg, nbd, src, tiles, tile_row, tile_col, tile_count):
    slots, tile = tiles.shape[:2]
    kcols = src.shape[1]
    block = min(64, slots)
    nin, nout = (2 * nbg, nbg) if forward else (nbg, 2 * nbg)
    sums = jax.ShapeDtypeStruct((nout, kcols, tile), jnp.bfloat16)
    own = jax.ShapeDtypeStruct((kcols, nbd * tile), jnp.bfloat16)
    own_spec = pl.BlockSpec((kcols, nbd * tile), lambda i, r, c, n: (0, 0))
    return pl.pallas_call(
        functools.partial(apply_kernel, forward, block, nbg),
        out_shape=sums if forward else (sums, own),
        grid_spec=pltpu.PrefetchScalarGridSpec(
            num_scalar_prefetch=3,
            grid=(slots // block,),
            in_specs=[
                ANY,
                pl.BlockSpec(
                    (block, tile, tile),
                    lambda i, r, c, n: (jnp.minimum(i, jnp.maximum(n[0] - 1, 0) // block), 0, 0)),
            ],
            out_specs=ANY if forward else (ANY, own_spec),
            scratch_shapes=[
                pltpu.VMEM((nout + 1, kcols, tile), jnp.float32),
                pltpu.VMEM((nin, kcols, tile), jnp.bfloat16),
                pltpu.VMEM((nout, kcols, tile), jnp.bfloat16),
                pltpu.SemaphoreType.DMA((1,)),
                pltpu.SemaphoreType.DMA((4,)),
            ],
        ),
        compiler_params=pltpu.CompilerParams(
            dimension_semantics=("arbitrary",), vmem_limit_bytes=VMEM_LIMIT),
        name="apply_forward" if forward else "apply_transposed",
    )(tile_row, tile_col, tile_count, src, tiles)


class Summed:
    def __init__(self, n, nbd, group, me, part, base, local, lsem, staged, landed, send, recv):
        self.n, self.nbd, self.group, self.me = n, nbd, group, me
        self.part, self.base, self.local, self.lsem = part, base, local, lsem
        self.staged, self.landed, self.send, self.recv = staged, landed, send, recv
        self.orders = sum_orders(n)

    def fetch(self, r):
        at = pl.ds(self.base + flip(self.me, r) * self.nbd, self.nbd)
        return pltpu.make_async_copy(self.part.at[at], self.local.at[r // 2], self.lsem.at[r // 2])

    def begin(self):
        for r in range(0, self.n, 2):
            self.fetch(r).start()

    def fetched(self):
        for r in range(0, self.n, 2):
            self.fetch(r).wait()

    def copy(self, chunk, r):
        order = self.orders[chunk]
        bit = [b for b in order if r & b][0]
        start, size = chunks_of(self.nbd)[chunk]
        if bit == order[0]:
            source = self.part.at[pl.ds(self.base + flip(self.me, r) * self.nbd + start, size)]
        else:
            source = self.staged.at[r, pl.ds(start, size)]
        return pltpu.make_async_remote_copy(
            src_ref=source, dst_ref=self.landed.at[r, pl.ds(start, size)],
            send_sem=self.send.at[chunk, r], recv_sem=self.recv.at[chunk, r],
            device_id=(self.group, flip(self.me, bit)), device_id_type=MESH)

    def sent_at(self, chunk, stage):
        order = self.orders[chunk]
        done = sum(order[:stage])
        rest = [r for r in range(self.n) if r & order[stage] and not r & done]

        def needed(r):
            later = [k for k, b in enumerate(order) if r & b and k > stage]
            return later[0] if later else len(order)

        return sorted(rest, key=needed)

    def value(self, chunk, r, stage, put, more=None):
        order = self.orders[chunk]
        start, size = chunks_of(self.nbd)[chunk]
        for bit in order[:stage]:
            self.copy(chunk, r | bit).wait_recv()
        for j in range(start, start + size):
            total = self.local[r // 2, j].astype(jnp.float32)
            for bit in order[:stage]:
                total = total + self.landed[r | bit, j].astype(jnp.float32)
            if more is not None:
                total = total + more[r // 2, j].astype(jnp.float32)
            put(j, total)

    def stage(self, stage, chunks, ready=None, more=None):
        for chunk in chunks:
            for r in self.sent_at(chunk, stage):
                if stage:
                    def put(j, total, r=r):
                        self.staged[r, j] = total.astype(jnp.bfloat16)
                    if ready is not None:
                        ready(chunk, r)
                    self.value(chunk, r, stage, put, more)
                self.copy(chunk, r).start()

    def finish(self, chunk, put, more=None):
        self.value(chunk, 0, len(self.orders[chunk]), put, more)

    def drain(self, first_stage_only=()):
        for chunk in range(CHUNKS):
            for r in range(1, self.n):
                if chunk not in first_stage_only or r & self.orders[chunk][0]:
                    self.copy(chunk, r).wait_send()


def reduce_kernel(n, groups, part, out, mine, local, psem, staged, landed, send, recv, gsend, grecv, lsem):
    group, me = lax.axis_index("grp"), lax.axis_index("narrow")
    nbd = mine.shape[0]
    greet(n, group, groups, me, False)
    summed = Summed(n, nbd, group, me, part, 0, local, psem, staged, landed, send, recv)
    every = range(CHUNKS)
    summed.stage(0, every)
    summed.begin()
    summed.fetched()
    for stage in range(1, len(bits_of(n))):
        summed.stage(stage, every)

    def put(j, total):
        mine[j] = total.astype(jnp.bfloat16)

    args = (n, nbd, group, me, mine, out, 0, gsend, grecv)
    for pair in range(0, CHUNKS, 2):
        for chunk in (pair, pair + 1):
            summed.finish(chunk, put)
        spread_own(args, (pair, pair + 1))
    keep = pltpu.make_async_copy(mine, out.at[pl.ds(me * nbd, nbd)], lsem.at[0])
    keep.start()
    for level in range(1, len(bits_of(n))):
        spread_level(args, level, every)
    spread_ends(args, every)
    summed.drain()
    spread_finish(*args, every)
    keep.wait()


def reduce_rows(n, groups, nbd, part):
    nbg, cols = part.shape[:2]
    return pl.pallas_call(
        functools.partial(reduce_kernel, n, groups),
        out_shape=jax.ShapeDtypeStruct((nbg, cols, 128), jnp.bfloat16),
        in_specs=[ANY],
        out_specs=VMEM,
        scratch_shapes=[
            pltpu.VMEM((nbd, cols, 128), jnp.bfloat16),
            pltpu.VMEM((n // 2, nbd, cols, 128), jnp.bfloat16),
            pltpu.SemaphoreType.DMA((n // 2,)),
            pltpu.VMEM((n, nbd, cols, 128), jnp.bfloat16),
            pltpu.VMEM((n, nbd, cols, 128), jnp.bfloat16),
            pltpu.SemaphoreType.DMA((CHUNKS, n)),
            pltpu.SemaphoreType.DMA((CHUNKS, n)),
            pltpu.SemaphoreType.DMA((CHUNKS, n)),
            pltpu.SemaphoreType.DMA((CHUNKS, n)),
            pltpu.SemaphoreType.DMA((1,)),
        ],
        compiler_params=pltpu.CompilerParams(
            collective_id=2, has_side_effects=True, vmem_limit_bytes=VMEM_LIMIT),
        name="reduce_rows",
    )(part)


def image_kernel(n, groups, part, out, plocal, olocal, pfetch, ofetch, pstaged, planded, ostaged, olanded,
                 psend, precv, osend, orecv, zstaged, zlanded, zsend, zrecv):
    group, me = lax.axis_index("grp"), lax.axis_index("narrow")
    nbd = zstaged.shape[1]
    stages = len(bits_of(n))
    greet(n, group, groups, me, True)
    prior = Summed(n, nbd, group, me, part, 0, plocal, pfetch, pstaged, planded, psend, precv)
    own = Summed(n, nbd, group, me, part, n * nbd, olocal, ofetch, ostaged, olanded, osend, orecv)

    def zcopy(chunk, r, target):
        at = pl.ds(*chunks_of(nbd)[chunk])
        return pltpu.make_async_remote_copy(
            src_ref=zstaged.at[r // 2, at], dst_ref=zlanded.at[r // 2, at],
            send_sem=zsend.at[chunk, r], recv_sem=zrecv.at[chunk, r],
            device_id=(target, me), device_id_type=MESH)

    def down(chunk, r, stage):
        def put(j, total):
            zstaged[r // 2, j] = total.astype(jnp.bfloat16)
        prior.value(chunk, r, stage, put)
        zcopy(chunk, r, group - 1).start()

    def ready(chunk, r):
        @pl.when(group < groups - 1)
        def _():
            zcopy(chunk, r, group + 1).wait_recv()

    @pl.when(group > 0)
    def _():
        prior.stage(0, ALONG + PLAIN)
        prior.begin()

    own.stage(0, PLAIN + ALONG)
    own.begin()

    @pl.when(group == groups - 1)
    def _():
        zlanded[...] = jnp.zeros_like(zlanded)

    @pl.when(group > 0)
    def _():
        prior.fetched()
        for r in sorted(range(0, n, 2), reverse=True):
            for chunk in ALONG:
                down(chunk, r, 1)
        prior.stage(1, PLAIN)

    own.fetched()
    own.stage(1, PLAIN)
    for stage in range(2, stages):
        @pl.when(group > 0)
        def _():
            prior.stage(stage, PLAIN)
    own.stage(1, ALONG, ready, zlanded)

    @pl.when(group > 0)
    def _():
        for chunk in PLAIN:
            down(chunk, 0, stages)

    for stage in range(2, stages):
        own.stage(stage, PLAIN)
        own.stage(stage, ALONG, ready, zlanded)

    def put_own(j, total):
        out[:, j * 128:(j + 1) * 128] = total

    for chunk in ALONG + PLAIN:
        ready(chunk, 0)
        own.finish(chunk, put_own, zlanded)

    own.drain()

    @pl.when(group > 0)
    def _():
        prior.drain(ALONG)
        for chunk in range(CHUNKS):
            for r in range(0, n, 2) if chunk in ALONG else (0,):
                zcopy(chunk, r, group - 1).wait_send()


def image(n, groups, nbd, part):
    cols = part.shape[1]
    held = pltpu.VMEM((n, nbd, cols, 128), jnp.bfloat16)
    evens = pltpu.VMEM((n // 2, nbd, cols, 128), jnp.bfloat16)
    fetch = pltpu.SemaphoreType.DMA((n // 2,))
    sems = pltpu.SemaphoreType.DMA((CHUNKS, n))
    return pl.pallas_call(
        functools.partial(image_kernel, n, groups),
        out_shape=jax.ShapeDtypeStruct((cols, nbd * 128), jnp.float32),
        in_specs=[ANY],
        out_specs=VMEM,
        scratch_shapes=[evens, evens, fetch, fetch, held, held, held, held, sems, sems, sems, sems,
                        evens, evens, sems, sems],
        compiler_params=pltpu.CompilerParams(
            collective_id=3, has_side_effects=True, vmem_limit_bytes=VMEM_LIMIT),
        name="image_sums",
    )(part)


def leave_kernel(sums, out):
    out[...] = sums[...]


def leave(sums):
    return pl.pallas_call(
        leave_kernel,
        out_shape=jax.ShapeDtypeStruct(sums.shape, sums.dtype),
        in_specs=[VMEM],
        out_specs=VMEM,
        compiler_params=pltpu.CompilerParams(vmem_limit_bytes=VMEM_LIMIT),
        name="leave",
    )(sums)


def body(panel, tiles, tile_row, tile_col, tile_count):
    tile = tiles.shape[1]
    nbd = panel.shape[1] // tile
    n, groups = lax.axis_size("narrow"), lax.axis_size("grp")
    nbg = nbd * n
    both = gather(n, groups, nbd, panel)
    part = apply_tiles(True, nbg, nbd, both, tiles, tile_row, tile_col, tile_count)
    rows = reduce_rows(n, groups, nbd, part)
    sums, filtered = apply_tiles(False, nbg, nbd, rows, tiles, tile_row, tile_col, tile_count)
    return filtered, leave(image(n, groups, nbd, sums))


def solution(mesh):
    spread = P(("grp", "narrow"))
    columns = P(None, ("grp", "narrow"))
    return jax.shard_map(
        body,
        mesh=mesh,
        in_specs=(columns, P(("grp", "narrow"), None, None), spread, spread, spread),
        out_specs=(columns, columns),
        check_vma=False,
    )
```

```python
import functools

import jax
import jax.numpy as jnp
from jax import lax
from jax.experimental import pallas as pl
from jax.experimental.pallas import tpu as pltpu
from jax.sharding import PartitionSpec as P

MESH = pl.DeviceIdType.MESH
VMEM_LIMIT = 56 * 1024 * 1024
BATCH = 64
DELAY = 4
CHUNKS = 4
PLAIN, ALONG = (0, 1), (2, 3)
ANY = pl.BlockSpec(memory_space=pl.ANY)
VMEM = pl.BlockSpec(memory_space=pltpu.VMEM)


def flip(index, mask):
    bit = 1
    while bit <= mask:
        if mask & bit:
            index = index + bit - 2 * bit * ((index // bit) % 2)
        bit *= 2
    return index


def bits_of(n):
    bits = []
    while 2 ** len(bits) < n:
        bits.append(2 ** len(bits))
    return bits


def spread_orders(n):
    bits = bits_of(n)
    return [bits[1:] + bits[:1], bits[:0:-1] + bits[:1]] * (CHUNKS // 2)


def sum_orders(n):
    bits = bits_of(n)
    return [bits[:1] + bits[1:], bits[:1] + bits[:0:-1]] * (CHUNKS // 2)


def chunks_of(nbd):
    big = -(-nbd // CHUNKS)
    edges = [0, big, 2 * big, 2 * big + (nbd - 2 * big) // 2, nbd]
    return [(low, high - low) for low, high in zip(edges, edges[1:])]


def greet(n, group, groups, me, along_grp):
    barrier = pltpu.get_barrier_semaphore()
    bits = bits_of(n)
    for bit in bits:
        pl.semaphore_signal(barrier, inc=1, device_id=(group, flip(me, bit)), device_id_type=MESH)
    if along_grp:
        @pl.when(group > 0)
        def _():
            pl.semaphore_signal(barrier, inc=1, device_id=(group - 1, me), device_id_type=MESH)

        @pl.when(group < groups - 1)
        def _():
            pl.semaphore_signal(barrier, inc=1, device_id=(group + 1, me), device_id_type=MESH)

        ends = jnp.minimum(group, 1) + jnp.minimum(groups - 1 - group, 1)
        pl.semaphore_wait(barrier, len(bits) + ends)
    else:
        pl.semaphore_wait(barrier, len(bits))


def spread_steps(n):
    steps = []
    for chunk, order in enumerate(spread_orders(n)):
        place = {bit: k for k, bit in enumerate(order)}
        for r in range(n):
            held = [place[bit] for bit in order if r & bit]
            last = max(held) if held else -1
            steps.append((len(held), chunk, r, order[last + 1:]))
    return [step[1:] for step in sorted(steps, key=lambda s: (s[0], s[1] // 2, -len(s[3]), s[2], s[1]))]


def spread_copy(n, nbd, group, me, own, out, base, send, recv, chunk, r, bit):
    start, size = chunks_of(nbd)[chunk]
    at = pl.ds(base + flip(me, r) * nbd + start, size)
    source = out.at[at] if r or own is None else own.at[pl.ds(start, size)]
    return pltpu.make_async_remote_copy(
        src_ref=source, dst_ref=out.at[at],
        send_sem=send.at[chunk, r | bit], recv_sem=recv.at[chunk, r | bit],
        device_id=(group, flip(me, bit)), device_id_type=MESH)


def spread_here(args, chunk, r):
    if r:
        last = [bit for bit in spread_orders(args[0])[chunk] if r & bit][-1]
        spread_copy(*args, chunk, r - last, last).wait_recv()


def spread_own(args, chunks):
    orders = spread_orders(args[0])
    for k in range(len(orders[0])):
        for chunk in chunks:
            spread_copy(*args, chunk, 0, orders[chunk][k]).start()


def spread_level(args, level, chunks, also=None):
    for chunk, r, sends in spread_steps(args[0]):
        if chunk in chunks and bin(r).count("1") == level and sends:
            spread_here(args, chunk, r)
            for bit in sends:
                spread_copy(*args, chunk, r, bit).start()
            if also is not None:
                also(chunk, r)


def spread_ends(args, chunks):
    for chunk, r, sends in spread_steps(args[0]):
        if chunk in chunks and r and not sends:
            spread_here(args, chunk, r)


def spread_finish(n, nbd, group, me, own, out, base, send, recv, chunks):
    copy = functools.partial(spread_copy, n, nbd, group, me, own, out, base, send, recv)
    for chunk, r, sends in spread_steps(n):
        for bit in sends if chunk in chunks else ():
            copy(chunk, r, bit).wait_send()


def gather_kernel(n, groups, panel, out, mine, send, recv, psend, precv, zsend, zrecv, lsem):
    group, me = lax.axis_index("grp"), lax.axis_index("narrow")
    nbd = mine.shape[0]
    nbg = n * nbd
    levels = len(bits_of(n))
    every = range(CHUNKS)
    evens = sorted(range(0, n, 2), key=lambda r: bin(r).count("1"))
    for j in range(nbd):
        mine[j] = panel[:, j * 128:(j + 1) * 128]
    greet(n, group, groups, me, True)

    def zcopy(chunk, r, target):
        start, size = chunks_of(nbd)[chunk]
        at = flip(me, r) * nbd + start
        source = out.at[pl.ds(nbg + at, size)] if r else mine.at[pl.ds(start, size)]
        return pltpu.make_async_remote_copy(
            src_ref=source, dst_ref=out.at[pl.ds(at, size)],
            send_sem=zsend.at[chunk, r], recv_sem=zrecv.at[chunk, r],
            device_id=(target, me), device_id_type=MESH)

    own = (n, nbd, group, me, mine, out, nbg, send, recv)
    prior = (n, nbd, group, me, None, out, 0, psend, precv)

    @pl.when(group < groups - 1)
    def _():
        for chunk in every:
            zcopy(chunk, 0, group + 1).start()

    spread_own(own, every)
    keep = pltpu.make_async_copy(mine, out.at[pl.ds(nbg + me * nbd, nbd)], lsem.at[0])
    keep.start()

    def up(chunk, r):
        if chunk in ALONG and r % 2 == 0:
            @pl.when(group < groups - 1)
            def _():
                zcopy(chunk, r, group + 1).start()

    for level in range(1, levels):
        spread_level(own, level, every, up)

        @pl.when(group > 0)
        def _():
            if level == 1:
                for chunk in PLAIN:
                    zcopy(chunk, 0, group - 1).wait_recv()
                spread_own(prior, PLAIN)
            for r in evens:
                if bin(r).count("1") == level - 1:
                    for chunk in ALONG:
                        zcopy(chunk, r, group - 1).wait_recv()
                        spread_copy(*prior, chunk, r, 1).start()

    @pl.when(group > 0)
    def _():
        for level in range(1, levels):
            spread_level(prior, level, PLAIN)
        for r in evens:
            if bin(r).count("1") >= levels - 1:
                for chunk in ALONG:
                    zcopy(chunk, r, group - 1).wait_recv()
                    spread_copy(*prior, chunk, r, 1).start()

    spread_ends(own, every)

    @pl.when(group > 0)
    def _():
        spread_ends(prior, PLAIN)
        spread_finish(*prior, PLAIN)
        for chunk in ALONG:
            for r in evens:
                spread_copy(*prior, chunk, r, 1).wait()

    spread_finish(*own, every)
    keep.wait()

    @pl.when(group < groups - 1)
    def _():
        for chunk in every:
            for r in evens if chunk in ALONG else (0,):
                zcopy(chunk, r, group + 1).wait_send()


def gather(n, groups, nbd, panel):
    cols = panel.shape[0]
    nbg = n * nbd
    return pl.pallas_call(
        functools.partial(gather_kernel, n, groups),
        out_shape=jax.ShapeDtypeStruct((2 * nbg, cols, 128), jnp.bfloat16),
        in_specs=[VMEM],
        out_specs=ANY,
        scratch_shapes=[
            pltpu.VMEM((nbd, cols, 128), jnp.bfloat16),
            pltpu.SemaphoreType.DMA((CHUNKS, n)),
            pltpu.SemaphoreType.DMA((CHUNKS, n)),
            pltpu.SemaphoreType.DMA((CHUNKS, n)),
            pltpu.SemaphoreType.DMA((CHUNKS, n)),
            pltpu.SemaphoreType.DMA((CHUNKS, n)),
            pltpu.SemaphoreType.DMA((CHUNKS, n)),
            pltpu.SemaphoreType.DMA((1,)),
        ],
        compiler_params=pltpu.CompilerParams(
            collective_id=1, has_side_effects=True, vmem_limit_bytes=VMEM_LIMIT),
        name="gather_panel",
    )(panel)


def apply_kernel(forward, block, nbg, rows, cols, count, src, tiles, *rest):
    if forward:
        out, acc = rest
    else:
        out, filtered, acc = rest
    step = pl.program_id(0)
    live = count[0]
    group = lax.axis_index("grp")
    row0, col0 = group * nbg, (group - 1) * nbg
    nout = out.shape[0]

    @pl.when(step == 0)
    def _():
        acc[...] = jnp.zeros_like(acc)
        if not forward:
            nbd = filtered.shape[1] // 128
            first_own = lax.axis_index("narrow") * nbd
            for j in range(nbd):
                filtered[:, j * 128:(j + 1) * 128] = src[first_own + j]

    first = step * block
    here = jnp.clip(live - first, 0, block)

    def batch(b, carry):
        waiting = []

        def add():
            place, prod = waiting.pop(0)
            acc[place] += prod

        for u in range(BATCH):
            at = b * BATCH + u
            slot = first + at
            row, col = rows[slot] - row0, cols[slot] - col0
            source, place = (col, row) if forward else (row, col)
            prod = lax.dot_general(
                src[source], tiles[at], (((1,), (1 if forward else 0,)), ((), ())),
                preferred_element_type=jnp.float32)
            waiting.append((jnp.where(slot < live, place, nout), prod))
            if len(waiting) > DELAY:
                add()
        while waiting:
            add()
        return carry

    lax.fori_loop(0, (here + BATCH - 1) // BATCH, batch, 0)

    @pl.when(step == pl.num_programs(0) - 1)
    def _():
        def put(j, carry):
            out[j] = acc[j].astype(out.dtype)
            return carry
        lax.fori_loop(0, nout, put, 0, unroll=8)


def apply_tiles(forward, nbg, nbd, src, tiles, tile_row, tile_col, tile_count):
    slots, tile = tiles.shape[:2]
    kcols = src.shape[1]
    block = min(64, slots)
    nin, nout = (2 * nbg, nbg) if forward else (nbg, 2 * nbg)
    whole = lambda i, r, c, n: (0, 0, 0)
    sums = jax.ShapeDtypeStruct((nout, kcols, tile), jnp.bfloat16)
    sums_spec = pl.BlockSpec((nout, kcols, tile), whole)
    own = jax.ShapeDtypeStruct((kcols, nbd * tile), jnp.bfloat16)
    own_spec = pl.BlockSpec((kcols, nbd * tile), lambda i, r, c, n: (0, 0))
    return pl.pallas_call(
        functools.partial(apply_kernel, forward, block, nbg),
        out_shape=sums if forward else (sums, own),
        grid_spec=pltpu.PrefetchScalarGridSpec(
            num_scalar_prefetch=3,
            grid=(slots // block,),
            in_specs=[
                pl.BlockSpec((nin, kcols, tile), whole),
                pl.BlockSpec(
                    (block, tile, tile),
                    lambda i, r, c, n: (jnp.minimum(i, jnp.maximum(n[0] - 1, 0) // block), 0, 0)),
            ],
            out_specs=sums_spec if forward else (sums_spec, own_spec),
            scratch_shapes=[pltpu.VMEM((nout + 1, kcols, tile), jnp.float32)],
        ),
        compiler_params=pltpu.CompilerParams(
            dimension_semantics=("arbitrary",), vmem_limit_bytes=VMEM_LIMIT),
        name="apply_forward" if forward else "apply_transposed",
    )(tile_row, tile_col, tile_count, src, tiles)


class Summed:
    def __init__(self, n, nbd, group, me, part, base, local, lsem, staged, landed, send, recv):
        self.n, self.nbd, self.group, self.me = n, nbd, group, me
        self.part, self.base, self.local, self.lsem = part, base, local, lsem
        self.staged, self.landed, self.send, self.recv = staged, landed, send, recv
        self.orders = sum_orders(n)

    def fetch(self, r):
        at = pl.ds(self.base + flip(self.me, r) * self.nbd, self.nbd)
        return pltpu.make_async_copy(self.part.at[at], self.local.at[r // 2], self.lsem.at[r // 2])

    def begin(self):
        for r in range(0, self.n, 2):
            self.fetch(r).start()

    def fetched(self):
        for r in range(0, self.n, 2):
            self.fetch(r).wait()

    def copy(self, chunk, r):
        order = self.orders[chunk]
        bit = [b for b in order if r & b][0]
        start, size = chunks_of(self.nbd)[chunk]
        if bit == order[0]:
            source = self.part.at[pl.ds(self.base + flip(self.me, r) * self.nbd + start, size)]
        else:
            source = self.staged.at[r, pl.ds(start, size)]
        return pltpu.make_async_remote_copy(
            src_ref=source, dst_ref=self.landed.at[r, pl.ds(start, size)],
            send_sem=self.send.at[chunk, r], recv_sem=self.recv.at[chunk, r],
            device_id=(self.group, flip(self.me, bit)), device_id_type=MESH)

    def sent_at(self, chunk, stage):
        order = self.orders[chunk]
        done = sum(order[:stage])
        rest = [r for r in range(self.n) if r & order[stage] and not r & done]

        def needed(r):
            later = [k for k, b in enumerate(order) if r & b and k > stage]
            return later[0] if later else len(order)

        return sorted(rest, key=needed)

    def value(self, chunk, r, stage, put, more=None):
        order = self.orders[chunk]
        start, size = chunks_of(self.nbd)[chunk]
        for bit in order[:stage]:
            self.copy(chunk, r | bit).wait_recv()
        for j in range(start, start + size):
            total = self.local[r // 2, j].astype(jnp.float32)
            for bit in order[:stage]:
                total = total + self.landed[r | bit, j].astype(jnp.float32)
            if more is not None:
                total = total + more[r // 2, j].astype(jnp.float32)
            put(j, total)

    def stage(self, stage, chunks, ready=None, more=None):
        for chunk in chunks:
            for r in self.sent_at(chunk, stage):
                if stage:
                    def put(j, total, r=r):
                        self.staged[r, j] = total.astype(jnp.bfloat16)
                    if ready is not None:
                        ready(chunk, r)
                    self.value(chunk, r, stage, put, more)
                self.copy(chunk, r).start()

    def finish(self, chunk, put, more=None):
        self.value(chunk, 0, len(self.orders[chunk]), put, more)

    def drain(self, first_stage_only=()):
        for chunk in range(CHUNKS):
            for r in range(1, self.n):
                if chunk not in first_stage_only or r & self.orders[chunk][0]:
                    self.copy(chunk, r).wait_send()


def reduce_kernel(n, groups, part, out, mine, local, psem, staged, landed, send, recv, gsend, grecv, lsem):
    group, me = lax.axis_index("grp"), lax.axis_index("narrow")
    nbd = mine.shape[0]
    greet(n, group, groups, me, False)
    summed = Summed(n, nbd, group, me, part, 0, local, psem, staged, landed, send, recv)
    every = range(CHUNKS)
    summed.stage(0, every)
    summed.begin()
    summed.fetched()
    for stage in range(1, len(bits_of(n))):
        summed.stage(stage, every)

    def put(j, total):
        mine[j] = total.astype(jnp.bfloat16)

    args = (n, nbd, group, me, mine, out, 0, gsend, grecv)
    for pair in range(0, CHUNKS, 2):
        for chunk in (pair, pair + 1):
            summed.finish(chunk, put)
        spread_own(args, (pair, pair + 1))
    keep = pltpu.make_async_copy(mine, out.at[pl.ds(me * nbd, nbd)], lsem.at[0])
    keep.start()
    for level in range(1, len(bits_of(n))):
        spread_level(args, level, every)
    spread_ends(args, every)
    summed.drain()
    spread_finish(*args, every)
    keep.wait()


def reduce_rows(n, groups, nbd, part):
    nbg, cols = part.shape[:2]
    return pl.pallas_call(
        functools.partial(reduce_kernel, n, groups),
        out_shape=jax.ShapeDtypeStruct((nbg, cols, 128), jnp.bfloat16),
        in_specs=[ANY],
        out_specs=ANY,
        scratch_shapes=[
            pltpu.VMEM((nbd, cols, 128), jnp.bfloat16),
            pltpu.VMEM((n // 2, nbd, cols, 128), jnp.bfloat16),
            pltpu.SemaphoreType.DMA((n // 2,)),
            pltpu.VMEM((n, nbd, cols, 128), jnp.bfloat16),
            pltpu.VMEM((n, nbd, cols, 128), jnp.bfloat16),
            pltpu.SemaphoreType.DMA((CHUNKS, n)),
            pltpu.SemaphoreType.DMA((CHUNKS, n)),
            pltpu.SemaphoreType.DMA((CHUNKS, n)),
            pltpu.SemaphoreType.DMA((CHUNKS, n)),
            pltpu.SemaphoreType.DMA((1,)),
        ],
        compiler_params=pltpu.CompilerParams(
            collective_id=2, has_side_effects=True, vmem_limit_bytes=VMEM_LIMIT),
        name="reduce_rows",
    )(part)


def image_kernel(n, groups, part, out, plocal, olocal, pfetch, ofetch, pstaged, planded, ostaged, olanded,
                 psend, precv, osend, orecv, zstaged, zlanded, zsend, zrecv):
    group, me = lax.axis_index("grp"), lax.axis_index("narrow")
    nbd = zstaged.shape[1]
    stages = len(bits_of(n))
    greet(n, group, groups, me, True)
    prior = Summed(n, nbd, group, me, part, 0, plocal, pfetch, pstaged, planded, psend, precv)
    own = Summed(n, nbd, group, me, part, n * nbd, olocal, ofetch, ostaged, olanded, osend, orecv)

    def zcopy(chunk, r, target):
        at = pl.ds(*chunks_of(nbd)[chunk])
        return pltpu.make_async_remote_copy(
            src_ref=zstaged.at[r // 2, at], dst_ref=zlanded.at[r // 2, at],
            send_sem=zsend.at[chunk, r], recv_sem=zrecv.at[chunk, r],
            device_id=(target, me), device_id_type=MESH)

    def down(chunk, r, stage):
        def put(j, total):
            zstaged[r // 2, j] = total.astype(jnp.bfloat16)
        prior.value(chunk, r, stage, put)
        zcopy(chunk, r, group - 1).start()

    def ready(chunk, r):
        @pl.when(group < groups - 1)
        def _():
            zcopy(chunk, r, group + 1).wait_recv()

    @pl.when(group > 0)
    def _():
        prior.stage(0, ALONG + PLAIN)
        prior.begin()

    own.stage(0, PLAIN + ALONG)
    own.begin()

    @pl.when(group == groups - 1)
    def _():
        zlanded[...] = jnp.zeros_like(zlanded)

    @pl.when(group > 0)
    def _():
        prior.fetched()
        for r in sorted(range(0, n, 2), reverse=True):
            for chunk in ALONG:
                down(chunk, r, 1)
        prior.stage(1, PLAIN)

    own.fetched()
    own.stage(1, PLAIN)
    for stage in range(2, stages):
        @pl.when(group > 0)
        def _():
            prior.stage(stage, PLAIN)
    own.stage(1, ALONG, ready, zlanded)

    @pl.when(group > 0)
    def _():
        for chunk in PLAIN:
            down(chunk, 0, stages)

    for stage in range(2, stages):
        own.stage(stage, PLAIN)
        own.stage(stage, ALONG, ready, zlanded)

    def put_own(j, total):
        out[:, j * 128:(j + 1) * 128] = total

    for chunk in ALONG + PLAIN:
        ready(chunk, 0)
        own.finish(chunk, put_own, zlanded)

    own.drain()

    @pl.when(group > 0)
    def _():
        prior.drain(ALONG)
        for chunk in range(CHUNKS):
            for r in range(0, n, 2) if chunk in ALONG else (0,):
                zcopy(chunk, r, group - 1).wait_send()


def image(n, groups, nbd, part):
    cols = part.shape[1]
    held = pltpu.VMEM((n, nbd, cols, 128), jnp.bfloat16)
    evens = pltpu.VMEM((n // 2, nbd, cols, 128), jnp.bfloat16)
    fetch = pltpu.SemaphoreType.DMA((n // 2,))
    sems = pltpu.SemaphoreType.DMA((CHUNKS, n))
    return pl.pallas_call(
        functools.partial(image_kernel, n, groups),
        out_shape=jax.ShapeDtypeStruct((cols, nbd * 128), jnp.float32),
        in_specs=[ANY],
        out_specs=VMEM,
        scratch_shapes=[evens, evens, fetch, fetch, held, held, held, held, sems, sems, sems, sems,
                        evens, evens, sems, sems],
        compiler_params=pltpu.CompilerParams(
            collective_id=3, has_side_effects=True, vmem_limit_bytes=VMEM_LIMIT),
        name="image_sums",
    )(part)


def body(panel, tiles, tile_row, tile_col, tile_count):
    tile = tiles.shape[1]
    nbd = panel.shape[1] // tile
    n, groups = lax.axis_size("narrow"), lax.axis_size("grp")
    nbg = nbd * n
    both = gather(n, groups, nbd, panel)
    part = apply_tiles(True, nbg, nbd, both, tiles, tile_row, tile_col, tile_count)
    rows = reduce_rows(n, groups, nbd, part)
    sums, filtered = apply_tiles(False, nbg, nbd, rows, tiles, tile_row, tile_col, tile_count)
    return filtered, image(n, groups, nbd, sums)


def solution(mesh):
    spread = P(("grp", "narrow"))
    columns = P(None, ("grp", "narrow"))
    return jax.shard_map(
        body,
        mesh=mesh,
        in_specs=(columns, P(("grp", "narrow"), None, None), spread, spread, spread),
        out_specs=(columns, columns),
        check_vma=False,
    )
```

```python
import functools

import jax
import jax.numpy as jnp
from jax import lax
from jax.experimental import pallas as pl
from jax.experimental.pallas import tpu as pltpu
from jax.sharding import PartitionSpec as P

MESH = pl.DeviceIdType.MESH
VMEM_LIMIT = 56 * 1024 * 1024
BATCH = 64
DELAY = 4
CHUNKS = 6
PLAIN, ALONG = (0, 1, 2, 3), (4, 5)
ANY = pl.BlockSpec(memory_space=pl.ANY)
VMEM = pl.BlockSpec(memory_space=pltpu.VMEM)


def flip(index, mask):
    bit = 1
    while bit <= mask:
        if mask & bit:
            index = index + bit - 2 * bit * ((index // bit) % 2)
        bit *= 2
    return index


def bits_of(n):
    bits = []
    while 2 ** len(bits) < n:
        bits.append(2 ** len(bits))
    return bits


def spread_orders(n):
    bits = bits_of(n)
    return [bits[1:] + bits[:1], bits[:0:-1] + bits[:1]] * (CHUNKS // 2)


def sum_orders(n):
    bits = bits_of(n)
    return [bits[:1] + bits[1:], bits[:1] + bits[:0:-1]] * (CHUNKS // 2)


def chunks_of(nbd):
    edges = [0]
    for k in range(CHUNKS):
        edges.append(edges[-1] + nbd // CHUNKS + (k >= CHUNKS - nbd % CHUNKS))
    return [(low, high - low) for low, high in zip(edges, edges[1:])]


def greet(n, group, groups, me, along_grp):
    barrier = pltpu.get_barrier_semaphore()
    bits = bits_of(n)
    for bit in bits:
        pl.semaphore_signal(barrier, inc=1, device_id=(group, flip(me, bit)), device_id_type=MESH)
    if along_grp:
        @pl.when(group > 0)
        def _():
            pl.semaphore_signal(barrier, inc=1, device_id=(group - 1, me), device_id_type=MESH)

        @pl.when(group < groups - 1)
        def _():
            pl.semaphore_signal(barrier, inc=1, device_id=(group + 1, me), device_id_type=MESH)

        ends = jnp.minimum(group, 1) + jnp.minimum(groups - 1 - group, 1)
        pl.semaphore_wait(barrier, len(bits) + ends)
    else:
        pl.semaphore_wait(barrier, len(bits))


def spread_steps(n):
    steps = []
    for chunk, order in enumerate(spread_orders(n)):
        place = {bit: k for k, bit in enumerate(order)}
        for r in range(n):
            held = [place[bit] for bit in order if r & bit]
            last = max(held) if held else -1
            steps.append((len(held), chunk, r, order[last + 1:]))
    return [step[1:] for step in sorted(steps, key=lambda s: (s[0], s[1] // 2, -len(s[3]), s[2], s[1]))]


def spread_copy(n, nbd, group, me, own, out, base, send, recv, chunk, r, bit):
    start, size = chunks_of(nbd)[chunk]
    at = pl.ds(base + flip(me, r) * nbd + start, size)
    source = out.at[at] if r or own is None else own.at[pl.ds(start, size)]
    return pltpu.make_async_remote_copy(
        src_ref=source, dst_ref=out.at[at],
        send_sem=send.at[chunk, r | bit], recv_sem=recv.at[chunk, r | bit],
        device_id=(group, flip(me, bit)), device_id_type=MESH)


def spread_here(args, chunk, r):
    if r:
        last = [bit for bit in spread_orders(args[0])[chunk] if r & bit][-1]
        spread_copy(*args, chunk, r - last, last).wait_recv()


def spread_own(args, chunks):
    orders = spread_orders(args[0])
    for k in range(len(orders[0])):
        for chunk in chunks:
            spread_copy(*args, chunk, 0, orders[chunk][k]).start()


def spread_level(args, level, chunks, also=None):
    for chunk, r, sends in spread_steps(args[0]):
        if chunk in chunks and bin(r).count("1") == level and sends:
            spread_here(args, chunk, r)
            for bit in sends:
                spread_copy(*args, chunk, r, bit).start()
            if also is not None:
                also(chunk, r)


def spread_ends(args, chunks):
    for chunk, r, sends in spread_steps(args[0]):
        if chunk in chunks and r and not sends:
            spread_here(args, chunk, r)


def spread_finish(n, nbd, group, me, own, out, base, send, recv, chunks):
    copy = functools.partial(spread_copy, n, nbd, group, me, own, out, base, send, recv)
    for chunk, r, sends in spread_steps(n):
        for bit in sends if chunk in chunks else ():
            copy(chunk, r, bit).wait_send()


def gather_kernel(n, groups, panel, out, mine, send, recv, psend, precv, zsend, zrecv, lsem):
    group, me = lax.axis_index("grp"), lax.axis_index("narrow")
    nbd = mine.shape[0]
    nbg = n * nbd
    levels = len(bits_of(n))
    every = range(CHUNKS)
    evens = sorted(range(0, n, 2), key=lambda r: bin(r).count("1"))
    for j in range(nbd):
        mine[j] = panel[:, j * 128:(j + 1) * 128]
    greet(n, group, groups, me, True)

    def zcopy(chunk, r, target):
        start, size = chunks_of(nbd)[chunk]
        at = flip(me, r) * nbd + start
        source = out.at[pl.ds(nbg + at, size)] if r else mine.at[pl.ds(start, size)]
        return pltpu.make_async_remote_copy(
            src_ref=source, dst_ref=out.at[pl.ds(at, size)],
            send_sem=zsend.at[chunk, r], recv_sem=zrecv.at[chunk, r],
            device_id=(target, me), device_id_type=MESH)

    own = (n, nbd, group, me, mine, out, nbg, send, recv)
    prior = (n, nbd, group, me, None, out, 0, psend, precv)

    @pl.when(group < groups - 1)
    def _():
        for chunk in every:
            zcopy(chunk, 0, group + 1).start()

    spread_own(own, every)
    keep = pltpu.make_async_copy(mine, out.at[pl.ds(nbg + me * nbd, nbd)], lsem.at[0])
    keep.start()

    def up(chunk, r):
        if chunk in ALONG and r % 2 == 0:
            @pl.when(group < groups - 1)
            def _():
                zcopy(chunk, r, group + 1).start()

    for level in range(1, levels):
        spread_level(own, level, every, up)

        @pl.when(group > 0)
        def _():
            if level == 1:
                for chunk in PLAIN:
                    zcopy(chunk, 0, group - 1).wait_recv()
                spread_own(prior, PLAIN)
            for r in evens:
                if bin(r).count("1") == level - 1:
                    for chunk in ALONG:
                        zcopy(chunk, r, group - 1).wait_recv()
                        spread_copy(*prior, chunk, r, 1).start()

    @pl.when(group > 0)
    def _():
        for level in range(1, levels):
            spread_level(prior, level, PLAIN)
        for r in evens:
            if bin(r).count("1") >= levels - 1:
                for chunk in ALONG:
                    zcopy(chunk, r, group - 1).wait_recv()
                    spread_copy(*prior, chunk, r, 1).start()

    spread_ends(own, every)

    @pl.when(group > 0)
    def _():
        spread_ends(prior, PLAIN)
        spread_finish(*prior, PLAIN)
        for chunk in ALONG:
            for r in evens:
                spread_copy(*prior, chunk, r, 1).wait()

    spread_finish(*own, every)
    keep.wait()

    @pl.when(group < groups - 1)
    def _():
        for chunk in every:
            for r in evens if chunk in ALONG else (0,):
                zcopy(chunk, r, group + 1).wait_send()


def gather(n, groups, nbd, panel):
    cols = panel.shape[0]
    nbg = n * nbd
    return pl.pallas_call(
        functools.partial(gather_kernel, n, groups),
        out_shape=jax.ShapeDtypeStruct((2 * nbg, cols, 128), jnp.bfloat16),
        in_specs=[VMEM],
        out_specs=ANY,
        scratch_shapes=[
            pltpu.VMEM((nbd, cols, 128), jnp.bfloat16),
            pltpu.SemaphoreType.DMA((CHUNKS, n)),
            pltpu.SemaphoreType.DMA((CHUNKS, n)),
            pltpu.SemaphoreType.DMA((CHUNKS, n)),
            pltpu.SemaphoreType.DMA((CHUNKS, n)),
            pltpu.SemaphoreType.DMA((CHUNKS, n)),
            pltpu.SemaphoreType.DMA((CHUNKS, n)),
            pltpu.SemaphoreType.DMA((1,)),
        ],
        compiler_params=pltpu.CompilerParams(
            collective_id=1, has_side_effects=True, vmem_limit_bytes=VMEM_LIMIT),
        name="gather_panel",
    )(panel)


def apply_kernel(forward, block, nbg, rows, cols, count, src, tiles, *rest):
    if forward:
        out, acc = rest
    else:
        out, filtered, acc = rest
    step = pl.program_id(0)
    live = count[0]
    group = lax.axis_index("grp")
    row0, col0 = group * nbg, (group - 1) * nbg
    nout = out.shape[0]

    @pl.when(step == 0)
    def _():
        acc[...] = jnp.zeros_like(acc)
        if not forward:
            nbd = filtered.shape[1] // 128
            first_own = lax.axis_index("narrow") * nbd
            for j in range(nbd):
                filtered[:, j * 128:(j + 1) * 128] = src[first_own + j]

    first = step * block
    here = jnp.clip(live - first, 0, block)

    def batch(b, carry):
        waiting = []

        def add():
            place, prod = waiting.pop(0)
            acc[place] += prod

        for u in range(BATCH):
            at = b * BATCH + u
            slot = first + at
            row, col = rows[slot] - row0, cols[slot] - col0
            source, place = (col, row) if forward else (row, col)
            prod = lax.dot_general(
                src[source], tiles[at], (((1,), (1 if forward else 0,)), ((), ())),
                preferred_element_type=jnp.float32)
            waiting.append((jnp.where(slot < live, place, nout), prod))
            if len(waiting) > DELAY:
                add()
        while waiting:
            add()
        return carry

    lax.fori_loop(0, (here + BATCH - 1) // BATCH, batch, 0)

    @pl.when(step == pl.num_programs(0) - 1)
    def _():
        def put(j, carry):
            out[j] = acc[j].astype(out.dtype)
            return carry
        lax.fori_loop(0, nout, put, 0, unroll=8)


def apply_tiles(forward, nbg, nbd, src, tiles, tile_row, tile_col, tile_count):
    slots, tile = tiles.shape[:2]
    kcols = src.shape[1]
    block = min(128, slots)
    nin, nout = (2 * nbg, nbg) if forward else (nbg, 2 * nbg)
    whole = lambda i, r, c, n: (0, 0, 0)
    sums = jax.ShapeDtypeStruct((nout, kcols, tile), jnp.bfloat16)
    sums_spec = pl.BlockSpec((nout, kcols, tile), whole)
    own = jax.ShapeDtypeStruct((kcols, nbd * tile), jnp.bfloat16)
    own_spec = pl.BlockSpec((kcols, nbd * tile), lambda i, r, c, n: (0, 0))
    return pl.pallas_call(
        functools.partial(apply_kernel, forward, block, nbg),
        out_shape=sums if forward else (sums, own),
        grid_spec=pltpu.PrefetchScalarGridSpec(
            num_scalar_prefetch=3,
            grid=(slots // block,),
            in_specs=[
                pl.BlockSpec((nin, kcols, tile), whole),
                pl.BlockSpec(
                    (block, tile, tile),
                    lambda i, r, c, n: (jnp.minimum(i, jnp.maximum(n[0] - 1, 0) // block), 0, 0)),
            ],
            out_specs=sums_spec if forward else (sums_spec, own_spec),
            scratch_shapes=[pltpu.VMEM((nout + 1, kcols, tile), jnp.float32)],
        ),
        compiler_params=pltpu.CompilerParams(
            dimension_semantics=("arbitrary",), vmem_limit_bytes=VMEM_LIMIT),
        name="apply_forward" if forward else "apply_transposed",
    )(tile_row, tile_col, tile_count, src, tiles)


class Summed:
    def __init__(self, n, nbd, group, me, part, base, local, lsem, staged, landed, send, recv):
        self.n, self.nbd, self.group, self.me = n, nbd, group, me
        self.part, self.base, self.local, self.lsem = part, base, local, lsem
        self.staged, self.landed, self.send, self.recv = staged, landed, send, recv
        self.orders = sum_orders(n)

    def fetch(self, r):
        at = pl.ds(self.base + flip(self.me, r) * self.nbd, self.nbd)
        return pltpu.make_async_copy(self.part.at[at], self.local.at[r // 2], self.lsem.at[r // 2])

    def begin(self):
        for r in range(0, self.n, 2):
            self.fetch(r).start()

    def fetched(self):
        for r in range(0, self.n, 2):
            self.fetch(r).wait()

    def copy(self, chunk, r):
        order = self.orders[chunk]
        bit = [b for b in order if r & b][0]
        start, size = chunks_of(self.nbd)[chunk]
        if bit == order[0]:
            source = self.part.at[pl.ds(self.base + flip(self.me, r) * self.nbd + start, size)]
        else:
            source = self.staged.at[r, pl.ds(start, size)]
        return pltpu.make_async_remote_copy(
            src_ref=source, dst_ref=self.landed.at[r, pl.ds(start, size)],
            send_sem=self.send.at[chunk, r], recv_sem=self.recv.at[chunk, r],
            device_id=(self.group, flip(self.me, bit)), device_id_type=MESH)

    def sent_at(self, chunk, stage):
        order = self.orders[chunk]
        done = sum(order[:stage])
        rest = [r for r in range(self.n) if r & order[stage] and not r & done]

        def needed(r):
            later = [k for k, b in enumerate(order) if r & b and k > stage]
            return later[0] if later else len(order)

        return sorted(rest, key=needed)

    def value(self, chunk, r, stage, put, more=None):
        order = self.orders[chunk]
        start, size = chunks_of(self.nbd)[chunk]
        for bit in order[:stage]:
            self.copy(chunk, r | bit).wait_recv()
        for j in range(start, start + size):
            total = self.local[r // 2, j].astype(jnp.float32)
            for bit in order[:stage]:
                total = total + self.landed[r | bit, j].astype(jnp.float32)
            if more is not None:
                total = total + more[r // 2, j].astype(jnp.float32)
            put(j, total)

    def stage(self, stage, chunks, ready=None, more=None):
        for chunk in chunks:
            for r in self.sent_at(chunk, stage):
                if stage:
                    def put(j, total, r=r):
                        self.staged[r, j] = total.astype(jnp.bfloat16)
                    if ready is not None:
                        ready(chunk, r)
                    self.value(chunk, r, stage, put, more)
                self.copy(chunk, r).start()

    def finish(self, chunk, put, more=None):
        self.value(chunk, 0, len(self.orders[chunk]), put, more)

    def drain(self, first_stage_only=()):
        for chunk in range(CHUNKS):
            for r in range(1, self.n):
                if chunk not in first_stage_only or r & self.orders[chunk][0]:
                    self.copy(chunk, r).wait_send()


def reduce_kernel(n, groups, part, out, mine, local, psem, staged, landed, send, recv, gsend, grecv, lsem):
    group, me = lax.axis_index("grp"), lax.axis_index("narrow")
    nbd = mine.shape[0]
    greet(n, group, groups, me, False)
    summed = Summed(n, nbd, group, me, part, 0, local, psem, staged, landed, send, recv)
    every = range(CHUNKS)
    summed.stage(0, every)
    summed.begin()
    summed.fetched()
    for stage in range(1, len(bits_of(n))):
        summed.stage(stage, every)

    def put(j, total):
        mine[j] = total.astype(jnp.bfloat16)

    args = (n, nbd, group, me, mine, out, 0, gsend, grecv)
    for pair in range(0, CHUNKS, 2):
        for chunk in (pair, pair + 1):
            summed.finish(chunk, put)
        spread_own(args, (pair, pair + 1))
    keep = pltpu.make_async_copy(mine, out.at[pl.ds(me * nbd, nbd)], lsem.at[0])
    keep.start()
    for level in range(1, len(bits_of(n))):
        spread_level(args, level, every)
    spread_ends(args, every)
    summed.drain()
    spread_finish(*args, every)
    keep.wait()


def reduce_rows(n, groups, nbd, part):
    nbg, cols = part.shape[:2]
    return pl.pallas_call(
        functools.partial(reduce_kernel, n, groups),
        out_shape=jax.ShapeDtypeStruct((nbg, cols, 128), jnp.bfloat16),
        in_specs=[ANY],
        out_specs=ANY,
        scratch_shapes=[
            pltpu.VMEM((nbd, cols, 128), jnp.bfloat16),
            pltpu.VMEM((n // 2, nbd, cols, 128), jnp.bfloat16),
            pltpu.SemaphoreType.DMA((n // 2,)),
            pltpu.VMEM((n, nbd, cols, 128), jnp.bfloat16),
            pltpu.VMEM((n, nbd, cols, 128), jnp.bfloat16),
            pltpu.SemaphoreType.DMA((CHUNKS, n)),
            pltpu.SemaphoreType.DMA((CHUNKS, n)),
            pltpu.SemaphoreType.DMA((CHUNKS, n)),
            pltpu.SemaphoreType.DMA((CHUNKS, n)),
            pltpu.SemaphoreType.DMA((1,)),
        ],
        compiler_params=pltpu.CompilerParams(
            collective_id=2, has_side_effects=True, vmem_limit_bytes=VMEM_LIMIT),
        name="reduce_rows",
    )(part)


def image_kernel(n, groups, part, out, plocal, olocal, pfetch, ofetch, pstaged, planded, ostaged, olanded,
                 psend, precv, osend, orecv, zstaged, zlanded, zsend, zrecv):
    group, me = lax.axis_index("grp"), lax.axis_index("narrow")
    nbd = zstaged.shape[1]
    stages = len(bits_of(n))
    greet(n, group, groups, me, True)
    prior = Summed(n, nbd, group, me, part, 0, plocal, pfetch, pstaged, planded, psend, precv)
    own = Summed(n, nbd, group, me, part, n * nbd, olocal, ofetch, ostaged, olanded, osend, orecv)

    def zcopy(chunk, r, target):
        at = pl.ds(*chunks_of(nbd)[chunk])
        return pltpu.make_async_remote_copy(
            src_ref=zstaged.at[r // 2, at], dst_ref=zlanded.at[r // 2, at],
            send_sem=zsend.at[chunk, r], recv_sem=zrecv.at[chunk, r],
            device_id=(target, me), device_id_type=MESH)

    def down(chunk, r, stage):
        def put(j, total):
            zstaged[r // 2, j] = total.astype(jnp.bfloat16)
        prior.value(chunk, r, stage, put)
        zcopy(chunk, r, group - 1).start()

    def ready(chunk, r):
        @pl.when(group < groups - 1)
        def _():
            zcopy(chunk, r, group + 1).wait_recv()

    @pl.when(group > 0)
    def _():
        prior.stage(0, ALONG + PLAIN)
        prior.begin()

    own.stage(0, PLAIN + ALONG)
    own.begin()

    @pl.when(group == groups - 1)
    def _():
        zlanded[...] = jnp.zeros_like(zlanded)

    @pl.when(group > 0)
    def _():
        prior.fetched()
        for r in sorted(range(0, n, 2), reverse=True):
            for chunk in ALONG:
                down(chunk, r, 1)
        prior.stage(1, PLAIN)

    own.fetched()
    own.stage(1, PLAIN)
    for stage in range(2, stages):
        @pl.when(group > 0)
        def _():
            prior.stage(stage, PLAIN)
    own.stage(1, ALONG, ready, zlanded)

    @pl.when(group > 0)
    def _():
        for chunk in PLAIN:
            down(chunk, 0, stages)

    for stage in range(2, stages):
        own.stage(stage, PLAIN)
        own.stage(stage, ALONG, ready, zlanded)

    def put_own(j, total):
        out[:, j * 128:(j + 1) * 128] = total

    for chunk in ALONG + PLAIN:
        ready(chunk, 0)
        own.finish(chunk, put_own, zlanded)

    own.drain()

    @pl.when(group > 0)
    def _():
        prior.drain(ALONG)
        for chunk in range(CHUNKS):
            for r in range(0, n, 2) if chunk in ALONG else (0,):
                zcopy(chunk, r, group - 1).wait_send()


def image(n, groups, nbd, part):
    cols = part.shape[1]
    held = pltpu.VMEM((n, nbd, cols, 128), jnp.bfloat16)
    evens = pltpu.VMEM((n // 2, nbd, cols, 128), jnp.bfloat16)
    fetch = pltpu.SemaphoreType.DMA((n // 2,))
    sems = pltpu.SemaphoreType.DMA((CHUNKS, n))
    return pl.pallas_call(
        functools.partial(image_kernel, n, groups),
        out_shape=jax.ShapeDtypeStruct((cols, nbd * 128), jnp.float32),
        in_specs=[ANY],
        out_specs=VMEM,
        scratch_shapes=[evens, evens, fetch, fetch, held, held, held, held, sems, sems, sems, sems,
                        evens, evens, sems, sems],
        compiler_params=pltpu.CompilerParams(
            collective_id=3, has_side_effects=True, vmem_limit_bytes=VMEM_LIMIT),
        name="image_sums",
    )(part)


def body(panel, tiles, tile_row, tile_col, tile_count):
    tile = tiles.shape[1]
    nbd = panel.shape[1] // tile
    n, groups = lax.axis_size("narrow"), lax.axis_size("grp")
    nbg = nbd * n
    both = gather(n, groups, nbd, panel)
    part = apply_tiles(True, nbg, nbd, both, tiles, tile_row, tile_col, tile_count)
    rows = reduce_rows(n, groups, nbd, part)
    sums, filtered = apply_tiles(False, nbg, nbd, rows, tiles, tile_row, tile_col, tile_count)
    return filtered, image(n, groups, nbd, sums)


def solution(mesh):
    spread = P(("grp", "narrow"))
    columns = P(None, ("grp", "narrow"))
    return jax.shard_map(
        body,
        mesh=mesh,
        in_specs=(columns, P(("grp", "narrow"), None, None), spread, spread, spread),
        out_specs=(columns, columns),
        check_vma=False,
    )
```

```python
import functools

import jax
import jax.numpy as jnp
from jax import lax
from jax.experimental import pallas as pl
from jax.experimental.pallas import tpu as pltpu
from jax.sharding import PartitionSpec as P

MESH = pl.DeviceIdType.MESH
VMEM_LIMIT = 56 * 1024 * 1024
BATCH = 64
DELAY = 4
CHUNKS = 4
IMAGE_CHUNKS = 6
PLAIN, ALONG = (0, 1), (2, 3)
ANY = pl.BlockSpec(memory_space=pl.ANY)
VMEM = pl.BlockSpec(memory_space=pltpu.VMEM)


IMAGE_PLAIN, IMAGE_ALONG = (2, 3, 4, 5), (0, 1)


def flip(index, mask):
    bit = 1
    while bit <= mask:
        if mask & bit:
            index = index + bit - 2 * bit * ((index // bit) % 2)
        bit *= 2
    return index


def bits_of(n):
    bits = []
    while 2 ** len(bits) < n:
        bits.append(2 ** len(bits))
    return bits


def spread_orders(n):
    bits = bits_of(n)
    return [bits[1:] + bits[:1], bits[:0:-1] + bits[:1]] * (CHUNKS // 2)


def sum_orders(n, count):
    bits = bits_of(n)
    return [bits[:1] + bits[1:], bits[:1] + bits[:0:-1]] * (count // 2)


def chunks_of(nbd, count=CHUNKS):
    edges = [0]
    for k in range(count):
        edges.append(edges[-1] + nbd // count + (k < nbd % count))
    return [(low, high - low) for low, high in zip(edges, edges[1:])]


def greet(n, group, groups, me, along_grp):
    barrier = pltpu.get_barrier_semaphore()
    bits = bits_of(n)
    for bit in bits:
        pl.semaphore_signal(barrier, inc=1, device_id=(group, flip(me, bit)), device_id_type=MESH)
    if along_grp:
        @pl.when(group > 0)
        def _():
            pl.semaphore_signal(barrier, inc=1, device_id=(group - 1, me), device_id_type=MESH)

        @pl.when(group < groups - 1)
        def _():
            pl.semaphore_signal(barrier, inc=1, device_id=(group + 1, me), device_id_type=MESH)

        ends = jnp.minimum(group, 1) + jnp.minimum(groups - 1 - group, 1)
        pl.semaphore_wait(barrier, len(bits) + ends)
    else:
        pl.semaphore_wait(barrier, len(bits))


def spread_steps(n):
    steps = []
    for chunk, order in enumerate(spread_orders(n)):
        place = {bit: k for k, bit in enumerate(order)}
        for r in range(n):
            held = [place[bit] for bit in order if r & bit]
            last = max(held) if held else -1
            steps.append((len(held), chunk, r, order[last + 1:]))
    return [step[1:] for step in sorted(steps, key=lambda s: (s[0], s[1] // 2, -len(s[3]), s[2], s[1]))]


def spread_copy(n, nbd, group, me, own, out, base, send, recv, chunk, r, bit):
    start, size = chunks_of(nbd)[chunk]
    at = pl.ds(base + flip(me, r) * nbd + start, size)
    source = out.at[at] if r or own is None else own.at[pl.ds(start, size)]
    return pltpu.make_async_remote_copy(
        src_ref=source, dst_ref=out.at[at],
        send_sem=send.at[chunk, r | bit], recv_sem=recv.at[chunk, r | bit],
        device_id=(group, flip(me, bit)), device_id_type=MESH)


def spread_here(args, chunk, r):
    if r:
        last = [bit for bit in spread_orders(args[0])[chunk] if r & bit][-1]
        spread_copy(*args, chunk, r - last, last).wait_recv()


def spread_own(args, chunks):
    orders = spread_orders(args[0])
    for k in range(len(orders[0])):
        for chunk in chunks:
            spread_copy(*args, chunk, 0, orders[chunk][k]).start()


def spread_level(args, level, chunks, also=None):
    for chunk, r, sends in spread_steps(args[0]):
        if chunk in chunks and bin(r).count("1") == level and sends:
            spread_here(args, chunk, r)
            for bit in sends:
                spread_copy(*args, chunk, r, bit).start()
            if also is not None:
                also(chunk, r)


def spread_ends(args, chunks):
    for chunk, r, sends in spread_steps(args[0]):
        if chunk in chunks and r and not sends:
            spread_here(args, chunk, r)


def spread_finish(n, nbd, group, me, own, out, base, send, recv, chunks):
    copy = functools.partial(spread_copy, n, nbd, group, me, own, out, base, send, recv)
    for chunk, r, sends in spread_steps(n):
        for bit in sends if chunk in chunks else ():
            copy(chunk, r, bit).wait_send()


def gather_kernel(n, groups, panel, out, mine, send, recv, psend, precv, zsend, zrecv, lsem):
    group, me = lax.axis_index("grp"), lax.axis_index("narrow")
    nbd = mine.shape[0]
    nbg = n * nbd
    levels = len(bits_of(n))
    every = range(CHUNKS)
    evens = sorted(range(0, n, 2), key=lambda r: bin(r).count("1"))
    for j in range(nbd):
        mine[j] = panel[:, j * 128:(j + 1) * 128]
    greet(n, group, groups, me, True)

    def zcopy(chunk, r, target):
        start, size = chunks_of(nbd)[chunk]
        at = flip(me, r) * nbd + start
        source = out.at[pl.ds(nbg + at, size)] if r else mine.at[pl.ds(start, size)]
        return pltpu.make_async_remote_copy(
            src_ref=source, dst_ref=out.at[pl.ds(at, size)],
            send_sem=zsend.at[chunk, r], recv_sem=zrecv.at[chunk, r],
            device_id=(target, me), device_id_type=MESH)

    own = (n, nbd, group, me, mine, out, nbg, send, recv)
    prior = (n, nbd, group, me, None, out, 0, psend, precv)

    @pl.when(group < groups - 1)
    def _():
        for chunk in every:
            zcopy(chunk, 0, group + 1).start()

    spread_own(own, every)
    keep = pltpu.make_async_copy(mine, out.at[pl.ds(nbg + me * nbd, nbd)], lsem.at[0])
    keep.start()

    def up(chunk, r):
        if chunk in ALONG and r % 2 == 0:
            @pl.when(group < groups - 1)
            def _():
                zcopy(chunk, r, group + 1).start()

    for level in range(1, levels):
        spread_level(own, level, every, up)

        @pl.when(group > 0)
        def _():
            if level == 1:
                for chunk in PLAIN:
                    zcopy(chunk, 0, group - 1).wait_recv()
                spread_own(prior, PLAIN)
            for r in evens:
                if bin(r).count("1") == level - 1:
                    for chunk in ALONG:
                        zcopy(chunk, r, group - 1).wait_recv()
                        spread_copy(*prior, chunk, r, 1).start()

    @pl.when(group > 0)
    def _():
        for level in range(1, levels):
            spread_level(prior, level, PLAIN)
        for r in evens:
            if bin(r).count("1") >= levels - 1:
                for chunk in ALONG:
                    zcopy(chunk, r, group - 1).wait_recv()
                    spread_copy(*prior, chunk, r, 1).start()

    spread_ends(own, every)

    @pl.when(group > 0)
    def _():
        spread_ends(prior, PLAIN)
        spread_finish(*prior, PLAIN)
        for chunk in ALONG:
            for r in evens:
                spread_copy(*prior, chunk, r, 1).wait()

    spread_finish(*own, every)
    keep.wait()

    @pl.when(group < groups - 1)
    def _():
        for chunk in every:
            for r in evens if chunk in ALONG else (0,):
                zcopy(chunk, r, group + 1).wait_send()


def gather(n, groups, nbd, panel):
    cols = panel.shape[0]
    nbg = n * nbd
    return pl.pallas_call(
        functools.partial(gather_kernel, n, groups),
        out_shape=jax.ShapeDtypeStruct((2 * nbg, cols, 128), jnp.bfloat16),
        in_specs=[VMEM],
        out_specs=ANY,
        scratch_shapes=[
            pltpu.VMEM((nbd, cols, 128), jnp.bfloat16),
            pltpu.SemaphoreType.DMA((CHUNKS, n)),
            pltpu.SemaphoreType.DMA((CHUNKS, n)),
            pltpu.SemaphoreType.DMA((CHUNKS, n)),
            pltpu.SemaphoreType.DMA((CHUNKS, n)),
            pltpu.SemaphoreType.DMA((CHUNKS, n)),
            pltpu.SemaphoreType.DMA((CHUNKS, n)),
            pltpu.SemaphoreType.DMA((1,)),
        ],
        compiler_params=pltpu.CompilerParams(
            collective_id=1, has_side_effects=True, vmem_limit_bytes=VMEM_LIMIT),
        name="gather_panel",
    )(panel)


def apply_kernel(forward, block, nbg, rows, cols, count, src, tiles, *rest):
    if forward:
        out, acc = rest
    else:
        out, filtered, acc = rest
    step = pl.program_id(0)
    live = count[0]
    group = lax.axis_index("grp")
    row0, col0 = group * nbg, (group - 1) * nbg
    nout = out.shape[0]

    @pl.when(step == 0)
    def _():
        acc[...] = jnp.zeros_like(acc)
        if not forward:
            nbd = filtered.shape[1] // 128
            first_own = lax.axis_index("narrow") * nbd
            for j in range(nbd):
                filtered[:, j * 128:(j + 1) * 128] = src[first_own + j]

    first = step * block
    here = jnp.clip(live - first, 0, block)

    def batch(b, carry):
        waiting = []

        def add():
            place, prod = waiting.pop(0)
            acc[place] += prod

        for u in range(BATCH):
            at = b * BATCH + u
            slot = first + at
            row, col = rows[slot] - row0, cols[slot] - col0
            source, place = (col, row) if forward else (row, col)
            prod = lax.dot_general(
                src[source], tiles[at], (((1,), (1 if forward else 0,)), ((), ())),
                preferred_element_type=jnp.float32)
            waiting.append((jnp.where(slot < live, place, nout), prod))
            if len(waiting) > DELAY:
                add()
        while waiting:
            add()
        return carry

    lax.fori_loop(0, (here + BATCH - 1) // BATCH, batch, 0)

    @pl.when(step == pl.num_programs(0) - 1)
    def _():
        def put(j, carry):
            out[j] = acc[j].astype(out.dtype)
            return carry
        lax.fori_loop(0, nout, put, 0, unroll=8)


def apply_tiles(forward, nbg, nbd, src, tiles, tile_row, tile_col, tile_count):
    slots, tile = tiles.shape[:2]
    kcols = src.shape[1]
    block = min(64 if forward else 128, slots)
    nin, nout = (2 * nbg, nbg) if forward else (nbg, 2 * nbg)
    whole = lambda i, r, c, n: (0, 0, 0)
    sums = jax.ShapeDtypeStruct((nout, kcols, tile), jnp.bfloat16)
    sums_spec = pl.BlockSpec((nout, kcols, tile), whole)
    own = jax.ShapeDtypeStruct((kcols, nbd * tile), jnp.bfloat16)
    own_spec = pl.BlockSpec((kcols, nbd * tile), lambda i, r, c, n: (0, 0))
    return pl.pallas_call(
        functools.partial(apply_kernel, forward, block, nbg),
        out_shape=sums if forward else (sums, own),
        grid_spec=pltpu.PrefetchScalarGridSpec(
            num_scalar_prefetch=3,
            grid=(slots // block,),
            in_specs=[
                pl.BlockSpec((nin, kcols, tile), whole),
                pl.BlockSpec(
                    (block, tile, tile),
                    lambda i, r, c, n: (jnp.minimum(i, jnp.maximum(n[0] - 1, 0) // block), 0, 0)),
            ],
            out_specs=sums_spec if forward else (sums_spec, own_spec),
            scratch_shapes=[pltpu.VMEM((nout + 1, kcols, tile), jnp.float32)],
        ),
        compiler_params=pltpu.CompilerParams(
            dimension_semantics=("arbitrary",), vmem_limit_bytes=VMEM_LIMIT),
        name="apply_forward" if forward else "apply_transposed",
    )(tile_row, tile_col, tile_count, src, tiles)


class Summed:
    def __init__(self, n, nbd, group, me, part, base, local, lsem, staged, landed, send, recv, count=CHUNKS):
        self.n, self.nbd, self.group, self.me = n, nbd, group, me
        self.part, self.base, self.local, self.lsem = part, base, local, lsem
        self.staged, self.landed, self.send, self.recv = staged, landed, send, recv
        self.count = count
        self.orders = sum_orders(n, count)

    def fetch(self, r):
        at = pl.ds(self.base + flip(self.me, r) * self.nbd, self.nbd)
        return pltpu.make_async_copy(self.part.at[at], self.local.at[r // 2], self.lsem.at[r // 2])

    def begin(self):
        for r in range(0, self.n, 2):
            self.fetch(r).start()

    def fetched(self):
        for r in range(0, self.n, 2):
            self.fetch(r).wait()

    def copy(self, chunk, r):
        order = self.orders[chunk]
        bit = [b for b in order if r & b][0]
        start, size = chunks_of(self.nbd, self.count)[chunk]
        if bit == order[0]:
            source = self.part.at[pl.ds(self.base + flip(self.me, r) * self.nbd + start, size)]
        else:
            source = self.staged.at[r, pl.ds(start, size)]
        return pltpu.make_async_remote_copy(
            src_ref=source, dst_ref=self.landed.at[r, pl.ds(start, size)],
            send_sem=self.send.at[chunk, r], recv_sem=self.recv.at[chunk, r],
            device_id=(self.group, flip(self.me, bit)), device_id_type=MESH)

    def sent_at(self, chunk, stage):
        order = self.orders[chunk]
        done = sum(order[:stage])
        rest = [r for r in range(self.n) if r & order[stage] and not r & done]

        def needed(r):
            later = [k for k, b in enumerate(order) if r & b and k > stage]
            return later[0] if later else len(order)

        return sorted(rest, key=needed)

    def value(self, chunk, r, stage, put, more=None):
        order = self.orders[chunk]
        start, size = chunks_of(self.nbd, self.count)[chunk]
        for bit in order[:stage]:
            self.copy(chunk, r | bit).wait_recv()
        for j in range(start, start + size):
            total = self.local[r // 2, j].astype(jnp.float32)
            for bit in order[:stage]:
                total = total + self.landed[r | bit, j].astype(jnp.float32)
            if more is not None:
                total = total + more[r // 2, j].astype(jnp.float32)
            put(j, total)

    def stage(self, stage, chunks, ready=None, more=None):
        for chunk in chunks:
            for r in self.sent_at(chunk, stage):
                if stage:
                    def put(j, total, r=r):
                        self.staged[r, j] = total.astype(jnp.bfloat16)
                    if ready is not None:
                        ready(chunk, r)
                    self.value(chunk, r, stage, put, more)
                self.copy(chunk, r).start()

    def finish(self, chunk, put, more=None):
        self.value(chunk, 0, len(self.orders[chunk]), put, more)

    def drain(self, first_stage_only=()):
        for chunk in range(self.count):
            for r in range(1, self.n):
                if chunk not in first_stage_only or r & self.orders[chunk][0]:
                    self.copy(chunk, r).wait_send()


def reduce_kernel(n, groups, part, out, mine, local, psem, staged, landed, send, recv, gsend, grecv, lsem):
    group, me = lax.axis_index("grp"), lax.axis_index("narrow")
    nbd = mine.shape[0]
    greet(n, group, groups, me, False)
    summed = Summed(n, nbd, group, me, part, 0, local, psem, staged, landed, send, recv)
    every = range(CHUNKS)
    summed.stage(0, every)
    summed.begin()
    summed.fetched()
    for stage in range(1, len(bits_of(n))):
        summed.stage(stage, every)

    def put(j, total):
        mine[j] = total.astype(jnp.bfloat16)

    args = (n, nbd, group, me, mine, out, 0, gsend, grecv)
    for pair in range(0, CHUNKS, 2):
        for chunk in (pair, pair + 1):
            summed.finish(chunk, put)
        spread_own(args, (pair, pair + 1))
    keep = pltpu.make_async_copy(mine, out.at[pl.ds(me * nbd, nbd)], lsem.at[0])
    keep.start()
    for level in range(1, len(bits_of(n))):
        spread_level(args, level, every)
    spread_ends(args, every)
    summed.drain()
    spread_finish(*args, every)
    keep.wait()


def reduce_rows(n, groups, nbd, part):
    nbg, cols = part.shape[:2]
    return pl.pallas_call(
        functools.partial(reduce_kernel, n, groups),
        out_shape=jax.ShapeDtypeStruct((nbg, cols, 128), jnp.bfloat16),
        in_specs=[ANY],
        out_specs=ANY,
        scratch_shapes=[
            pltpu.VMEM((nbd, cols, 128), jnp.bfloat16),
            pltpu.VMEM((n // 2, nbd, cols, 128), jnp.bfloat16),
            pltpu.SemaphoreType.DMA((n // 2,)),
            pltpu.VMEM((n, nbd, cols, 128), jnp.bfloat16),
            pltpu.VMEM((n, nbd, cols, 128), jnp.bfloat16),
            pltpu.SemaphoreType.DMA((CHUNKS, n)),
            pltpu.SemaphoreType.DMA((CHUNKS, n)),
            pltpu.SemaphoreType.DMA((CHUNKS, n)),
            pltpu.SemaphoreType.DMA((CHUNKS, n)),
            pltpu.SemaphoreType.DMA((1,)),
        ],
        compiler_params=pltpu.CompilerParams(
            collective_id=2, has_side_effects=True, vmem_limit_bytes=VMEM_LIMIT),
        name="reduce_rows",
    )(part)


def image_kernel(n, groups, part, out, plocal, olocal, pfetch, ofetch, pstaged, planded, ostaged, olanded,
                 psend, precv, osend, orecv, zstaged, zlanded, zsend, zrecv):
    group, me = lax.axis_index("grp"), lax.axis_index("narrow")
    nbd = zstaged.shape[1]
    stages = len(bits_of(n))
    greet(n, group, groups, me, True)
    prior = Summed(n, nbd, group, me, part, 0, plocal, pfetch, pstaged, planded, psend, precv, IMAGE_CHUNKS)
    own = Summed(n, nbd, group, me, part, n * nbd, olocal, ofetch, ostaged, olanded, osend, orecv, IMAGE_CHUNKS)

    def zcopy(chunk, r, target):
        at = pl.ds(*chunks_of(nbd, IMAGE_CHUNKS)[chunk])
        return pltpu.make_async_remote_copy(
            src_ref=zstaged.at[r // 2, at], dst_ref=zlanded.at[r // 2, at],
            send_sem=zsend.at[chunk, r], recv_sem=zrecv.at[chunk, r],
            device_id=(target, me), device_id_type=MESH)

    def down(chunk, r, stage):
        def put(j, total):
            zstaged[r // 2, j] = total.astype(jnp.bfloat16)
        prior.value(chunk, r, stage, put)
        zcopy(chunk, r, group - 1).start()

    def ready(chunk, r):
        @pl.when(group < groups - 1)
        def _():
            zcopy(chunk, r, group + 1).wait_recv()

    @pl.when(group > 0)
    def _():
        prior.stage(0, IMAGE_ALONG + IMAGE_PLAIN)
        prior.begin()

    own.stage(0, IMAGE_PLAIN + IMAGE_ALONG)
    own.begin()

    @pl.when(group == groups - 1)
    def _():
        zlanded[...] = jnp.zeros_like(zlanded)

    @pl.when(group > 0)
    def _():
        prior.fetched()
        for r in sorted(range(0, n, 2), reverse=True):
            for chunk in IMAGE_ALONG:
                down(chunk, r, 1)
        prior.stage(1, IMAGE_PLAIN)

    own.fetched()
    own.stage(1, IMAGE_PLAIN)
    for stage in range(2, stages):
        @pl.when(group > 0)
        def _():
            prior.stage(stage, IMAGE_PLAIN)
    own.stage(1, IMAGE_ALONG, ready, zlanded)

    @pl.when(group > 0)
    def _():
        for chunk in IMAGE_PLAIN:
            down(chunk, 0, stages)

    for stage in range(2, stages):
        own.stage(stage, IMAGE_PLAIN)
        own.stage(stage, IMAGE_ALONG, ready, zlanded)

    def put_own(j, total):
        out[:, j * 128:(j + 1) * 128] = total

    for chunk in IMAGE_ALONG + IMAGE_PLAIN:
        ready(chunk, 0)
        own.finish(chunk, put_own, zlanded)

    own.drain()

    @pl.when(group > 0)
    def _():
        prior.drain(IMAGE_ALONG)
        for chunk in range(IMAGE_CHUNKS):
            for r in range(0, n, 2) if chunk in IMAGE_ALONG else (0,):
                zcopy(chunk, r, group - 1).wait_send()


def image(n, groups, nbd, part):
    cols = part.shape[1]
    held = pltpu.VMEM((n, nbd, cols, 128), jnp.bfloat16)
    evens = pltpu.VMEM((n // 2, nbd, cols, 128), jnp.bfloat16)
    fetch = pltpu.SemaphoreType.DMA((n // 2,))
    sems = pltpu.SemaphoreType.DMA((IMAGE_CHUNKS, n))
    return pl.pallas_call(
        functools.partial(image_kernel, n, groups),
        out_shape=jax.ShapeDtypeStruct((cols, nbd * 128), jnp.float32),
        in_specs=[ANY],
        out_specs=VMEM,
        scratch_shapes=[evens, evens, fetch, fetch, held, held, held, held, sems, sems, sems, sems,
                        evens, evens, sems, sems],
        compiler_params=pltpu.CompilerParams(
            collective_id=3, has_side_effects=True, vmem_limit_bytes=VMEM_LIMIT),
        name="image_sums",
    )(part)


def body(panel, tiles, tile_row, tile_col, tile_count):
    tile = tiles.shape[1]
    nbd = panel.shape[1] // tile
    n, groups = lax.axis_size("narrow"), lax.axis_size("grp")
    nbg = nbd * n
    both = gather(n, groups, nbd, panel)
    part = apply_tiles(True, nbg, nbd, both, tiles, tile_row, tile_col, tile_count)
    rows = reduce_rows(n, groups, nbd, part)
    sums, filtered = apply_tiles(False, nbg, nbd, rows, tiles, tile_row, tile_col, tile_count)
    return filtered, image(n, groups, nbd, sums)


def solution(mesh):
    spread = P(("grp", "narrow"))
    columns = P(None, ("grp", "narrow"))
    return jax.shard_map(
        body,
        mesh=mesh,
        in_specs=(columns, P(("grp", "narrow"), None, None), spread, spread, spread),
        out_specs=(columns, columns),
        check_vma=False,
    )
```
